128 devices in a mesh: band: 8 (over z, core), mesh: 16 (over x, y).
Axes of the slice: x: 4, y: 4, z: 4, core: 2. Of those that a mesh axis runs over, the one named last changes fastest.
Arguments:
- grid: bfloat16 [65536, 512], P(('band', 'mesh')), may hold values from -6 to 6
- mesh_latent: bfloat16 [32768, 512], P(('band', 'mesh')), may hold values from -6 to 6
- edge_latent: bfloat16 [262144, 512], P(('band', 'mesh')), may hold values from -6 to 6
- edge_grid_block: int32 [2048], P(('band', 'mesh')), may hold values from 0 to 63
- edge_mesh_block: int32 [2048], P(('band', 'mesh')), may hold values from 0 to 15
- sender_offset: int32 [2048, 128], P(('band', 'mesh')), may hold values from 0 to 127
- receiver_offset: int32 [2048, 128], P(('band', 'mesh')), may hold values from 0 to 127
- live_groups: int32 [128], P(('band', 'mesh')), may hold values from 1 to 4, as said below
- w_grid: bfloat16 [512, 512], replicated, may hold values from -0.25 to 0.25
- w_mesh: bfloat16 [512, 512], replicated, may hold values from -0.25 to 0.25
- w_edge: bfloat16 [512, 512], replicated, may hold values from -0.25 to 0.25
- bias: float32 [512], replicated, may hold values from -3 to 3
- w_out: bfloat16 [512, 512], replicated, may hold values from -0.25 to 0.25
- w_node: bfloat16 [512, 512], replicated, may hold values from -0.25 to 0.25
- cotangent: bfloat16 [32768, 512], P(('band', 'mesh')), may hold values from -6 to 6
Outputs:
- mesh_out: bfloat16 [32768, 512], P(('band', 'mesh'))
- grid_grad: float32 [65536, 512], P(('band', 'mesh'))
The draws below stay inside these ranges and needn't reach their ends.
Inputs may be any that keep to these rules, and one draw needn't show every extreme that they name: `live_groups`: each device has at least one live group, and some device has all 4 live.
All inputs are finite; a program needn't handle non-finite values.
Results may differ from the reference program's by a relative error of at most 0.0055.
Values may be sent and summed in bfloat16 or wider, within the bound.
No kernel may reach another device: no remote copies, remote signals or barrier semaphores. Data moves between devices by JAX's collectives and lax.ppermute only.
A program may use at most 128 MiB of HBM per device.

```python
import jax
import jax.numpy as jnp
from jax import lax

L = 512
G_DEV = 512
M_DEV = 256
EB_DEV = 16
GROUP = 4
GROUPS = 4
DEVS = 128
GB = 64
MB = 16
GRID = 65536
MESH = 32768
BLOCKS = 2048
EDGES = 262144
N_MESH = 16


def draw_live_groups(key, part):
    key = jax.random.fold_in(key, 7)
    first, second = jax.random.split(key)
    counts = jax.random.randint(first, (DEVS,), 1, GROUPS + 1)
    chosen = jax.random.randint(second, (), 0, DEVS)
    return jnp.where(jnp.arange(DEVS) == chosen, GROUPS, counts).astype(jnp.int32)


def plant(drawn, key, least, largest):
    longest = drawn.shape.index(max(drawn.shape))
    spots = []
    for shift in (0, 1):
        where = [jax.random.randint(jax.random.fold_in(key, axis), (), 0, length) for axis, length in enumerate(drawn.shape)]
        where[longest] = (where[longest] + shift) % drawn.shape[longest]
        spots.append(tuple(where))
    return drawn.at[spots[0]].set(least).at[spots[1]].set(largest)


def level_of(rng, shape, pieces, smallest, top_value):
    loudness, own = 1.0, jax.random.fold_in(rng, 6)
    for position, blocks in pieces:
        draws = jnp.exp(jax.random.uniform(jax.random.fold_in(own, position), (blocks,), jnp.float32, smallest / len(pieces), top_value / len(pieces)))
        loudness = loudness * jnp.repeat(draws, shape[position] // blocks).reshape([-1 if axis == position else 1 for axis in range(len(shape))])
    return loudness


def centred(stream_key, extent, width, bound, cuts=(), kind=jnp.bfloat16):
    array = jax.random.normal(stream_key, extent, jnp.float32) * width
    if len(cuts) > 0:
        array = level_of(stream_key, extent, cuts, -0.22, 0.18) * array
    return jnp.clip(array, min=-bound, max=bound).astype(kind)


def setup_inputs(seed: int = 0) -> dict:
    key_of = jax.random.split(jax.random.key(seed), 16)
    return {
        "grid": centred(key_of[0], (GRID, L), 1.0, 6.0, ((0, 128),)),
        "mesh_latent": centred(key_of[1], (MESH, L), 1.0, 6.0, ((0, 128),)),
        "edge_latent": centred(key_of[2], (EDGES, L), 1.0, 6.0, ((0, 128),)),
        "edge_grid_block": plant(jax.random.randint(key_of[3], (BLOCKS,), 0, GB), jax.random.fold_in(key_of[3], 1), 0, GB - 1).astype(jnp.int32),
        "edge_mesh_block": plant(jax.random.randint(key_of[4], (BLOCKS,), 0, MB), jax.random.fold_in(key_of[4], 1), 0, MB - 1).astype(jnp.int32),
        "sender_offset": plant(jax.random.randint(key_of[5], (BLOCKS, 128), 0, 128), jax.random.fold_in(key_of[5], 1), 0, 127).astype(jnp.int32),
        "receiver_offset": plant(jax.random.randint(key_of[6], (BLOCKS, 128), 0, 128), jax.random.fold_in(key_of[6], 1), 0, 127).astype(jnp.int32),
        "live_groups": draw_live_groups(jax.random.fold_in(key_of[15], 71), 0),
        "w_grid": centred(key_of[8], (L, L), L ** -0.5, 0.25),
        "w_mesh": centred(key_of[9], (L, L), L ** -0.5, 0.25),
        "w_edge": centred(key_of[10], (L, L), L ** -0.5, 0.25),
        "bias": centred(key_of[11], (L,), 0.5, 3.0, (), jnp.float32),
        "w_out": centred(key_of[12], (L, L), L ** -0.5, 0.25),
        "w_node": centred(key_of[13], (L, L), L ** -0.5, 0.25),
        "cotangent": centred(key_of[14], (MESH, L), 1.0, 6.0, ((0, 128),)),
    }


def silu_slope(value):
    sig = jax.nn.sigmoid(value)
    return sig * (1.0 + value * (1.0 - sig))


def reference(grid, mesh_latent, edge_latent, edge_grid_block, edge_mesh_block, sender_offset, receiver_offset, live_groups, w_grid, w_mesh, w_edge, bias, w_out, w_node, cotangent):
    band_rows = G_DEV * N_MESH

    def edge_terms(device):
        band_index = device // N_MESH
        mesh_index = device % N_MESH
        start = (device * EB_DEV).astype(jnp.int32)
        grid_blocks = lax.dynamic_slice_in_dim(edge_grid_block, start, EB_DEV)
        mesh_blocks = lax.dynamic_slice_in_dim(edge_mesh_block, start, EB_DEV)
        send_off = lax.dynamic_slice_in_dim(sender_offset, start, EB_DEV)
        recv_off = lax.dynamic_slice_in_dim(receiver_offset, start, EB_DEV)
        senders = (band_index * band_rows + grid_blocks[:, None] * 128 + send_off).reshape(-1).astype(jnp.int32)
        local_rows = (mesh_blocks[:, None] * 128 + recv_off).reshape(-1)
        receivers = (((local_rows // M_DEV) * N_MESH + mesh_index) * M_DEV + local_rows % M_DEV).astype(jnp.int32)
        slots = jnp.arange(EB_DEV * 128, dtype=jnp.int32) // (128 * GROUP)
        live = (slots < live_groups[device]).astype(jnp.float32)
        edges = lax.dynamic_slice_in_dim(edge_latent, (start * 128).astype(jnp.int32), EB_DEV * 128)
        pre = jnp.dot(grid[senders], w_grid, preferred_element_type=jnp.float32)
        pre = pre + jnp.dot(mesh_latent[receivers], w_mesh, preferred_element_type=jnp.float32)
        pre = pre + jnp.dot(edges, w_edge, preferred_element_type=jnp.float32) + bias
        return senders, receivers, live, pre

    def forward(total, device):
        senders, receivers, live, pre = edge_terms(device)
        hidden = jax.nn.silu(pre).astype(jnp.bfloat16)
        message = jnp.dot(hidden, w_out, preferred_element_type=jnp.float32) * live[:, None]
        return total.at[receivers].add(message), None

    devices = jnp.arange(DEVS, dtype=jnp.int32)
    aggregate, unused = lax.scan(forward, jnp.zeros((MESH, L), jnp.float32), devices)
    activation = jax.nn.silu(aggregate).astype(jnp.bfloat16)
    mesh_out = (mesh_latent.astype(jnp.float32) + jnp.dot(activation, w_node, preferred_element_type=jnp.float32)).astype(jnp.bfloat16)
    d_aggregate = (jnp.dot(cotangent, w_node.T, preferred_element_type=jnp.float32) * silu_slope(aggregate)).astype(jnp.bfloat16)

    def backward(total, device):
        senders, receivers, live, pre = edge_terms(device)
        d_hidden = jnp.dot(d_aggregate[receivers], w_out.T, preferred_element_type=jnp.float32)
        d_pre = (d_hidden * silu_slope(pre) * live[:, None]).astype(jnp.bfloat16)
        return total.at[senders].add(jnp.dot(d_pre, w_grid.T, preferred_element_type=jnp.float32)), None

    grid_grad, unused = lax.scan(backward, jnp.zeros((GRID, L), jnp.float32), devices)
    return mesh_out, grid_grad
```

```python
import functools

import jax
import jax.numpy as jnp
from jax import lax
from jax.experimental import pallas as pl
from jax.experimental.pallas import tpu as pltpu
from jax.sharding import Mesh
from jax.sharding import PartitionSpec as P

F32 = jnp.float32
BF16 = jnp.bfloat16
RING = 4
BLOCK = 128
SLOTS = 16
GROUP = 4
WIDTH = 512
CHUNKS = 2
COLS = WIDTH // CHUNKS
HALF = 256
GATHERED = RING * HALF
VMEM = pl.BlockSpec(memory_space=pltpu.VMEM)
SMEM = pl.BlockSpec(memory_space=pltpu.SMEM)
ANY = pl.BlockSpec(memory_space=pl.ANY)
LIMIT = 48 * 1024 * 1024


def shape(rows, cols, dtype):
    return jax.ShapeDtypeStruct((rows, cols), dtype)


def params():
    return pltpu.CompilerParams(vmem_limit_bytes=LIMIT)


CHIP_AXES = ("core", "x", "y")


def along(first, step):
    pairs = []
    for core in range(2):
        for x in range(RING):
            for y in range(RING):
                if (core == 0) == first:
                    to = ((x + step) % RING, y)
                else:
                    to = (x, (y + step) % RING)
                pairs.append((core * 16 + x * RING + y, core * 16 + to[0] * RING + to[1]))
    return pairs


def shift(value, first, step):
    return lax.ppermute(value, CHIP_AXES, along(first, step))


def shift_z(value, step):
    return lax.ppermute(value, "z", [(i, (i + step) % RING) for i in range(RING)])


def swap(value):
    return lax.ppermute(value, "core", [(0, 1), (1, 0)])


def dot(a, b):
    return jnp.dot(a, b, preferred_element_type=F32)


def dot_t(a, b):
    return lax.dot_general(a, b, (((1,), (1,)), ((), ())), preferred_element_type=F32)


def t_dot(a, b):
    return lax.dot_general(a, b, (((0,), (0,)), ((), ())), preferred_element_type=F32)


def split_dot(a, b, product):
    high = a.astype(BF16)
    low = (a - high.astype(F32)).astype(BF16)
    return product(high, b) + product(low, b)


def sigmoid(value):
    return 1.0 / (1.0 + jnp.exp(-value))


def one_hot(offsets, slot):
    rows = lax.broadcasted_iota(jnp.int32, (BLOCK, BLOCK), 0)
    return (rows == offsets[pl.ds(slot, 1), :]).astype(BF16)


def grid_place(block, where):
    core, x, y = where[1], where[2], where[3]
    owner = block // 4
    kind = (block % 4) // 2
    dx = lax.rem(x - owner // 4 + RING, RING)
    dy = lax.rem(y - owner % 4 + RING, RING)
    mine = kind == core
    near = jnp.where(kind == 0, dx, dy)
    far = jnp.where(kind == 0, dy, dx)
    return mine, near, far, (block % 2) * BLOCK


def mesh_place(block, where):
    owner = block // 2
    dz = lax.rem(owner // 2 - where[0] + RING, RING)
    return owner % 2 == where[1], dz, (block % 2) * BLOCK


def first_product_kernel(where, grid, w_grid, *outs):
    core = where[1]
    keep = grid[pl.ds(pl.multiple_of(core * HALF, HALF), HALF), :]
    give = grid[pl.ds(pl.multiple_of((1 - core) * HALF, HALF), HALF), :]
    for chunk in range(CHUNKS):
        cols = pl.ds(chunk * COLS, COLS)
        outs[2 * chunk][...] = dot(keep, w_grid[:, cols]).astype(BF16)
        outs[2 * chunk + 1][...] = dot(give, w_grid[:, cols]).astype(BF16)


def edge_kernel(where, live, mesh_block, recv, edge, w_mesh, w_edge, bias, *rest):
    pieces, outs, rows = rest[:8], rest[8 : 8 + CHUNKS], rest[-1]
    group = pl.program_id(0)

    @pl.when(group < live[0])
    def _():
        for i in range(GROUP):
            slot = group * GROUP + i
            mine, dz, row = mesh_place(mesh_block[slot], where)
            hot = one_hot(recv, slot)
            for piece in range(8):

                @pl.when(jnp.logical_and(mine == (piece < 4), dz == piece % 4))
                def _():
                    rows[pl.ds(i * BLOCK, BLOCK), :] = t_dot(hot, pieces[piece][pl.ds(pl.multiple_of(row, BLOCK), BLOCK), :]).astype(BF16)

        total = dot(rows[...], w_mesh[...]) + dot(edge[...], w_edge[...]) + bias[...]
        for chunk in range(CHUNKS):
            outs[chunk][...] = total[:, chunk * COLS : (chunk + 1) * COLS]


def forward_kernel(where, live, grid_block, mesh_block, send, recv, rest_in, *rest):
    pieces, (slope, near, far) = rest[:8], rest[8:11]
    total, blocks, sems = rest[11:]
    group = pl.program_id(0)

    def copies(slot, act):
        mine, first, second, row = grid_place(grid_block[slot], where)
        start = first * HALF + row
        for piece in range(8):

            @pl.when(jnp.logical_and(mine == (piece < 4), second == piece % 4))
            def _():
                act(pltpu.make_async_copy(pieces[piece].at[pl.ds(pl.multiple_of(start, BLOCK), BLOCK), :], blocks.at[slot], sems.at[slot]))

    @pl.when(group == 0)
    def _():
        @pl.loop(0, live[0] * GROUP)
        def _(slot):
            copies(slot, lambda copy: copy.start())

        total[...] = jnp.zeros_like(total)

    @pl.when(group < live[0])
    def _():
        hidden = []
        for i in range(GROUP):
            slot = group * GROUP + i
            pltpu.make_async_copy(pieces[0].at[pl.ds(0, BLOCK), :], blocks.at[slot], sems.at[slot]).wait()
            lines = pl.ds(i * BLOCK, BLOCK)
            pre = rest_in[lines, :] + t_dot(one_hot(send, slot), blocks[slot])
            sig = sigmoid(pre)
            slope[lines, :] = sig * (1.0 + pre * (1.0 - sig))
            hidden.append((pre * sig).astype(BF16))
        for i in range(GROUP):
            slot = group * GROUP + i
            mine, dz, row = mesh_place(mesh_block[slot], where)
            start = jnp.where(mine, 0, RING * HALF) + dz * HALF + row
            lines = pl.ds(pl.multiple_of(start, BLOCK), BLOCK)
            total[lines, :] += dot(one_hot(recv, slot), hidden[i])

    @pl.when(group == SLOTS // GROUP - 1)
    def _():
        near[...] = total[: RING * HALF, :]
        far[...] = total[RING * HALF :, :].astype(BF16)


def pair_sum_kernel(near, other, own, *outs):
    own[...] = near[:HALF, :] + other[:HALF, :].astype(F32)
    for step in range(1, RING):
        lines = pl.ds(step * HALF, HALF)
        outs[step - 1][...] = (near[lines, :] + other[lines, :].astype(F32)).astype(BF16)


def node_kernel(cot, w_out, *rest):
    sums, (aggregate, *grads) = rest[: 4 * CHUNKS], rest[4 * CHUNKS :]
    total = jnp.zeros((HALF, WIDTH), F32)
    for chunk in range(CHUNKS):
        own, a, b, c = sums[4 * chunk : 4 * chunk + 4]
        part = own[...] + (a[...].astype(F32) + b[...].astype(F32) + c[...].astype(F32))
        total += split_dot(part, w_out[pl.ds(chunk * COLS, COLS), :], dot)
    aggregate[...] = total
    sig = sigmoid(total)
    grad = (cot[...] * (sig * (1.0 + total * (1.0 - sig)))).astype(BF16)
    for chunk in range(CHUNKS):
        grads[chunk][...] = dot_t(grad, w_out[pl.ds(chunk * COLS, COLS), :]).astype(BF16)


def backward_kernel(where, live, grid_block, mesh_block, first_of, send, recv, slope, *rest):
    pieces, outs, (total, blocks) = rest[:8], rest[8:16], rest[16:]
    group = pl.program_id(0)

    @pl.when(group == 0)
    def _():
        for out in outs:
            out[...] = jnp.zeros_like(out)

    @pl.when(group < live[0])
    def _():
        for i in range(GROUP):
            slot = group * GROUP + i
            mine, dz, row = mesh_place(mesh_block[slot], where)
            for piece in range(8):

                @pl.when(jnp.logical_and(mine == (piece < 4), dz == piece % 4))
                def _():
                    blocks[i] = pieces[piece][pl.ds(pl.multiple_of(row, BLOCK), BLOCK), :]

        parts = []
        for i in range(GROUP):
            slot = group * GROUP + i
            grad = t_dot(one_hot(recv, slot), blocks[i]) * slope[pl.ds(i * BLOCK, BLOCK), :]
            parts.append(dot(one_hot(send, slot), grad.astype(BF16)))
        for i in range(GROUP):
            slot = group * GROUP + i
            first = first_of[slot]

            @pl.when(first == slot)
            def _():
                total[slot] = parts[i]

            @pl.when(first != slot)
            def _():
                total[first] += parts[i]

    @pl.when(group == SLOTS // GROUP - 1)
    def _():
        @pl.loop(0, live[0] * GROUP)
        def _(slot):
            @pl.when(first_of[slot] == slot)
            def _():
                mine, near, far, row = grid_place(grid_block[slot], where)
                near = lax.rem(RING - near, RING)
                far = lax.rem(RING - far, RING)
                lines = pl.ds(pl.multiple_of(near * HALF + row, BLOCK), BLOCK)
                for piece in range(8):

                    @pl.when(jnp.logical_and(mine == (piece < 4), far == piece % 4))
                    def _():
                        outs[piece][lines, :] = total[slot].astype(BF16)


def add(a, b):
    return (a[...].astype(F32) + b[...].astype(F32)).astype(BF16)


def merge_kernel(up, other_up, into_up, down, other_down, into_down, out_up, out_down):
    out_up[:GATHERED, :] = add(up, into_up)
    out_up[GATHERED:, :] = other_up[...]
    out_down[:GATHERED, :] = down[...]
    out_down[GATHERED:, :] = add(other_down, into_down)


def column_sum_kernel(own, other, up, down, here, *outs):
    for half, term in enumerate((own, other)):
        for step in range(RING):
            lines = pl.ds(step * HALF, HALF)
            both = pl.ds(half * GATHERED + step * HALF, HALF)
            value = term[lines, :].astype(F32) + (up[both, :].astype(F32) + down[both, :].astype(F32))
            place = pl.ds(half * HALF, HALF)
            if step == 0:
                here[place, :] = value
            else:
                outs[step - 1][place, :] = value.astype(BF16)


def row_sum_kernel(here, up, down, across, own, other):
    value = here[...] + (up[...].astype(F32) + down[...].astype(F32) + across[...].astype(F32))
    own[...] = value[:HALF, :]
    other[...] = value[HALF:, :]


def grid_grad_kernel(where, w_grid, *rest):
    out = rest[-1]
    core = where[1]
    for which in range(2):
        value = jnp.zeros((HALF, WIDTH), F32)
        for chunk in range(CHUNKS):
            value += split_dot(rest[2 * chunk + which][...], w_grid[:, chunk * COLS : (chunk + 1) * COLS], dot_t)
        place = core if which == 0 else 1 - core
        out[pl.ds(pl.multiple_of(place * HALF, HALF), HALF), :] = value


def per_device(
    grid,
    mesh_latent,
    edge_latent,
    edge_grid_block,
    edge_mesh_block,
    sender_offset,
    receiver_offset,
    live_groups,
    w_grid,
    w_mesh,
    w_edge,
    bias,
    w_out,
    w_node,
    cotangent,
):
    where = jnp.stack([lax.axis_index(a) for a in ("z", "core", "x", "y")]).astype(jnp.int32)
    edges = SLOTS * BLOCK
    groups = SLOTS // GROUP
    per_group = GROUP * BLOCK
    offsets = pl.BlockSpec((SLOTS, BLOCK), lambda i: (0, 0))
    whole = pl.BlockSpec((HALF, COLS), lambda i: (0, 0))

    products = pl.pallas_call(
        first_product_kernel,
        in_specs=[SMEM, VMEM, VMEM],
        out_specs=[VMEM] * (2 * CHUNKS),
        out_shape=[shape(HALF, COLS, BF16)] * (2 * CHUNKS),
        compiler_params=params(),
        name="first_product",
    )(where, grid, w_grid)

    def gather_grid(chunk):
        keep, give = products[2 * chunk], products[2 * chunk + 1]
        mine = jnp.concatenate([keep, swap(give)], axis=0)
        up, down, across = shift(mine, True, 1), shift(mine, True, -1), shift(mine, True, 2)
        ring = (mine, up, across, down)
        both = jnp.concatenate([p[:HALF] for p in ring] + [p[HALF:] for p in ring], axis=0)
        far_up, far_down = shift(both, False, 1), shift(both, False, -1)
        own_across = shift(far_up[:GATHERED], False, 1)
        other_across = shift(far_down[GATHERED:], False, -1)
        own = [both, far_up, own_across, far_down]
        other = [swap(both[GATHERED:]), swap(far_up[GATHERED:]), swap(other_across), swap(far_down[GATHERED:])]
        return own + other

    mesh_ring = [mesh_latent, shift_z(mesh_latent, -1), shift_z(mesh_latent, 2), shift_z(mesh_latent, 1)]
    mesh_pieces = mesh_ring + [swap(p) for p in mesh_ring]
    edge_terms = pl.pallas_call(
        edge_kernel,
        grid=(groups,),
        in_specs=[
            SMEM,
            SMEM,
            SMEM,
            offsets,
            pl.BlockSpec((per_group, WIDTH), lambda i: (i, 0)),
            pl.BlockSpec((WIDTH, WIDTH), lambda i: (0, 0)),
            pl.BlockSpec((WIDTH, WIDTH), lambda i: (0, 0)),
            pl.BlockSpec((1, WIDTH), lambda i: (0, 0)),
        ]
        + [pl.BlockSpec((HALF, WIDTH), lambda i: (0, 0))] * 8,
        out_specs=[pl.BlockSpec((per_group, COLS), lambda i: (i, 0))] * CHUNKS,
        out_shape=[shape(edges, COLS, F32)] * CHUNKS,
        scratch_shapes=[pltpu.VMEM((per_group, WIDTH), BF16)],
        compiler_params=params(),
        name="edge_terms",
    )(where, live_groups, edge_mesh_block, receiver_offset, edge_latent, w_mesh, w_edge, bias.reshape(1, WIDTH), *mesh_pieces)

    cot = dot_t(cotangent, w_node)

    def forward(chunk, pieces):
        return pl.pallas_call(
            forward_kernel,
            grid=(groups,),
            in_specs=[SMEM] * 4 + [offsets, offsets, pl.BlockSpec((per_group, COLS), lambda i: (i, 0))] + [ANY] * 8,
            out_specs=[
                pl.BlockSpec((per_group, COLS), lambda i: (i, 0)),
                pl.BlockSpec((RING * HALF, COLS), lambda i: (0, 0)),
                pl.BlockSpec((RING * HALF, COLS), lambda i: (0, 0)),
            ],
            out_shape=[shape(edges, COLS, F32), shape(RING * HALF, COLS, F32), shape(RING * HALF, COLS, BF16)],
            scratch_shapes=[
                pltpu.VMEM((2 * RING * HALF, COLS), F32),
                pltpu.VMEM((SLOTS, BLOCK, COLS), BF16),
                pltpu.SemaphoreType.DMA((SLOTS,)),
            ],
            compiler_params=params(),
            name=f"forward_{chunk}",
        )(where, live_groups, edge_grid_block, edge_mesh_block, sender_offset, receiver_offset, edge_terms[chunk], *pieces)

    def band_sum(chunk, near, far):
        own, a, b, c = pl.pallas_call(
            pair_sum_kernel,
            in_specs=[VMEM] * 2,
            out_specs=[VMEM] * 4,
            out_shape=[shape(HALF, COLS, F32)] + [shape(HALF, COLS, BF16)] * 3,
            compiler_params=params(),
            name=f"pair_sum_{chunk}",
        )(near, swap(far))
        return [own, shift_z(a, 1), shift_z(c, -1), shift_z(b, 2)]

    sums, slopes = [], []
    for chunk in range(CHUNKS):
        slope, near, far = forward(chunk, gather_grid(chunk))
        slopes.append(slope)
        sums += band_sum(chunk, near, far)

    aggregate, *grads = pl.pallas_call(
        node_kernel,
        in_specs=[VMEM] * (2 + 4 * CHUNKS),
        out_specs=[VMEM] * (1 + CHUNKS),
        out_shape=[shape(HALF, WIDTH, F32)] + [shape(HALF, COLS, BF16)] * CHUNKS,
        compiler_params=params(),
        name="node",
    )(cot, w_out, *sums)

    slots = jnp.arange(SLOTS)
    same = edge_grid_block[:, None] == edge_grid_block[None, :]
    first_of = jnp.min(jnp.where(same, slots[None, :], SLOTS), axis=1).astype(jnp.int32)

    def backward(chunk):
        ring = [grads[chunk], shift_z(grads[chunk], -1), shift_z(grads[chunk], 2), shift_z(grads[chunk], 1)]
        pieces = ring + [swap(p) for p in ring]
        return pl.pallas_call(
            backward_kernel,
            grid=(groups,),
            in_specs=[SMEM] * 5 + [offsets, offsets, pl.BlockSpec((per_group, COLS), lambda i: (i, 0))] + [whole] * 8,
            out_specs=[pl.BlockSpec((GATHERED, COLS), lambda i: (0, 0))] * 8,
            out_shape=[shape(GATHERED, COLS, BF16)] * 8,
            scratch_shapes=[pltpu.VMEM((SLOTS, BLOCK, COLS), F32), pltpu.VMEM((GROUP, BLOCK, COLS), BF16)],
            compiler_params=params(),
            name=f"backward_{chunk}",
        )(where, live_groups, edge_grid_block, edge_mesh_block, first_of, sender_offset, receiver_offset, slopes[chunk], *pieces)

    def scatter_grid(chunk, partial):
        own, other = partial[:4], [swap(p) for p in partial[4:]]
        into_up, into_down = shift(own[2], False, 1), shift(other[2], False, -1)
        up, down = pl.pallas_call(
            merge_kernel,
            in_specs=[VMEM] * 6,
            out_specs=[VMEM] * 2,
            out_shape=[shape(2 * GATHERED, COLS, BF16)] * 2,
            compiler_params=params(),
            name=f"merge_{chunk}",
        )(own[1], other[1], into_up, own[3], other[3], into_down)
        here, a, b, c = pl.pallas_call(
            column_sum_kernel,
            in_specs=[VMEM] * 4,
            out_specs=[VMEM] * 4,
            out_shape=[shape(2 * HALF, COLS, F32)] + [shape(2 * HALF, COLS, BF16)] * 3,
            compiler_params=params(),
            name=f"column_sum_{chunk}",
        )(own[0], other[0], shift(up, False, 1), shift(down, False, -1))
        mine, give = pl.pallas_call(
            row_sum_kernel,
            in_specs=[VMEM] * 4,
            out_specs=[VMEM] * 2,
            out_shape=[shape(HALF, COLS, F32)] * 2,
            compiler_params=params(),
            name=f"row_sum_{chunk}",
        )(here, shift(a, True, 1), shift(c, True, -1), shift(b, True, 2))
        return [mine, swap(give)]

    parts = []
    for chunk in range(CHUNKS):
        parts += scatter_grid(chunk, backward(chunk))

    grid_grad = pl.pallas_call(
        grid_grad_kernel,
        in_specs=[SMEM, VMEM] + [VMEM] * (2 * CHUNKS),
        out_specs=VMEM,
        out_shape=shape(2 * HALF, WIDTH, F32),
        compiler_params=params(),
        name="grid_grad",
    )(where, w_grid, *parts)

    activation = jax.nn.silu(aggregate).astype(BF16)
    mesh_out = (mesh_latent.astype(F32) + dot(activation, w_node)).astype(BF16)
    return (mesh_out, grid_grad)


def solution(mesh):
    split = Mesh(mesh.devices.reshape(4, 2, 4, 4), ("z", "core", "x", "y"))
    rows = P(("z", "core", "x", "y"))
    placed = (rows,) * 8 + (P(),) * 6 + (rows,)
    return jax.shard_map(per_device, mesh=split, in_specs=placed, out_specs=(rows, rows), check_vma=False)
```

```python
import functools

import jax
import jax.numpy as jnp
from jax import lax
from jax.experimental import pallas as pl
from jax.experimental.pallas import tpu as pltpu
from jax.sharding import Mesh
from jax.sharding import PartitionSpec as P

F32 = jnp.float32
BF16 = jnp.bfloat16
RING = 4
BLOCK = 128
SLOTS = 16
GROUP = 4
WIDTH = 512
CHUNKS = 2
COLS = WIDTH // CHUNKS
HALF = 256
GATHERED = RING * HALF
VMEM = pl.BlockSpec(memory_space=pltpu.VMEM)
SMEM = pl.BlockSpec(memory_space=pltpu.SMEM)
ANY = pl.BlockSpec(memory_space=pl.ANY)
LIGHT = pl.CostEstimate(flops=0, bytes_accessed=0, transcendentals=0)
LIMIT = 20 * 1024 * 1024


def shape(rows, cols, dtype):
    return jax.ShapeDtypeStruct((rows, cols), dtype)


def params():
    return pltpu.CompilerParams(vmem_limit_bytes=LIMIT)


CHIP_AXES = ("core", "x", "y")


def along(first, step):
    pairs = []
    for core in range(2):
        for x in range(RING):
            for y in range(RING):
                if (core == 0) == first:
                    to = ((x + step) % RING, y)
                else:
                    to = (x, (y + step) % RING)
                pairs.append((core * 16 + x * RING + y, core * 16 + to[0] * RING + to[1]))
    return pairs


def shift(value, first, step):
    return lax.ppermute(value, CHIP_AXES, along(first, step))


def shift_z(value, step):
    return lax.ppermute(value, "z", [(i, (i + step) % RING) for i in range(RING)])


def after(value, *others):
    return lax.optimization_barrier((value, others))[0]


def pair_z(value, flip):
    return lax.ppermute(value, "z", [(i, i ^ flip) for i in range(RING)])


def swap(value):
    return lax.ppermute(value, "core", [(0, 1), (1, 0)])


def dot(a, b):
    return jnp.dot(a, b, preferred_element_type=F32)


def dot_t(a, b):
    return lax.dot_general(a, b, (((1,), (1,)), ((), ())), preferred_element_type=F32)


def t_dot(a, b):
    return lax.dot_general(a, b, (((0,), (0,)), ((), ())), preferred_element_type=F32)


def split_dot(a, b, product):
    high = a.astype(BF16)
    low = (a - high.astype(F32)).astype(BF16)
    return product(high, b) + product(low, b)


def sigmoid(value):
    return 1.0 / (1.0 + jnp.exp(-value))


def one_hot(offsets, slot):
    rows = lax.broadcasted_iota(jnp.int32, (BLOCK, BLOCK), 0)
    return (rows == offsets[pl.ds(slot, 1), :]).astype(BF16)


def grid_place(block, where):
    core, x, y = where[1], where[2], where[3]
    owner = block // 4
    kind = (block % 4) // 2
    dx = lax.rem(x - owner // 4 + RING, RING)
    dy = lax.rem(y - owner % 4 + RING, RING)
    mine = kind == core
    near = jnp.where(kind == 0, dx, dy)
    far = jnp.where(kind == 0, dy, dx)
    return mine, near, far, (block % 2) * BLOCK


def mesh_place(block, where):
    owner = block // 2
    dz = lax.rem(owner // 2 - where[0] + RING, RING)
    return owner % 2 == where[1], dz, (block % 2) * BLOCK


def first_product_kernel(where, grid, w_grid, keep, give):
    core = where[1]
    for out, half in ((give, 1 - core), (keep, core)):
        out[...] = dot(grid[pl.ds(pl.multiple_of(half * HALF, HALF), HALF), :], w_grid[...]).astype(BF16)


def ring_kernel(keep, got, up, across, down, *outs):
    for chunk, out in enumerate(outs):
        cols = pl.ds(chunk * COLS, COLS)
        out[:HALF, :] = keep[:, cols]
        out[GATHERED : GATHERED + HALF, :] = got[:, cols]
        for step, term in enumerate((up, across, down)):
            out[pl.ds((step + 1) * HALF, HALF), :] = term[:HALF, cols]
            out[pl.ds(GATHERED + (step + 1) * HALF, HALF), :] = term[HALF:, cols]


def edge_kernel(where, live, mesh_block, recv, edge, w_mesh, w_edge, bias, *rest):
    pieces, outs, (blocks, rows) = rest[:2], rest[2 : 2 + CHUNKS], rest[-2:]

    @pl.loop(0, live[0])
    def _(group):
        for i in range(GROUP):
            block = mesh_block[group * GROUP + i]
            owner = block // 2
            flip = (owner // 2) ^ where[0]
            mine, far = owner % 2 == where[1], flip // 2
            row = (2 * far + (flip ^ (3 * far))) * HALF + (block % 2) * BLOCK
            for piece in range(2):

                @pl.when(mine == (piece == 0))
                def _():
                    blocks[i] = pieces[piece][pl.ds(pl.multiple_of(row, BLOCK), BLOCK), :]

        for i in range(GROUP):
            rows[pl.ds(i * BLOCK, BLOCK), :] = t_dot(one_hot(recv, group * GROUP + i), blocks[i]).astype(BF16)
        lines = pl.ds(pl.multiple_of(group * GROUP * BLOCK, GROUP * BLOCK), GROUP * BLOCK)
        for chunk in range(CHUNKS):
            cols = pl.ds(chunk * COLS, COLS)
            outs[chunk][lines, :] = dot(rows[...], w_mesh[:, cols]) + dot(edge[lines, :], w_edge[:, cols]) + bias[:, cols]


def forward_kernel(where, live, grid_block, mesh_block, send, recv, rest_in, *rest):
    pieces, (slope, near, far) = rest[:6], rest[6:9]
    total, blocks, sems = rest[9:]

    @pl.loop(0, live[0] * GROUP)
    def _(slot):
        mine, first, second, row = grid_place(grid_block[slot], where)
        start = first * HALF + row
        for piece in range(6):
            if piece < RING:
                here, base = jnp.logical_and(mine, second == piece), 0
            elif piece == RING:
                here, base = jnp.logical_and(jnp.logical_not(mine), second != 2), jnp.minimum(second, 2) * GATHERED
            else:
                here, base = jnp.logical_and(jnp.logical_not(mine), second == 2), 0

            @pl.when(here)
            def _():
                lines = pl.ds(pl.multiple_of(base + start, BLOCK), BLOCK)
                pltpu.make_async_copy(pieces[piece].at[lines, :], blocks.at[slot], sems.at[slot]).start()

    total[...] = jnp.zeros_like(total)

    @pl.loop(0, live[0])
    def _(group):
        hidden = []
        for i in range(GROUP):
            slot = group * GROUP + i
            pltpu.make_async_copy(pieces[0].at[pl.ds(0, BLOCK), :], blocks.at[slot], sems.at[slot]).wait()
            lines = pl.ds(pl.multiple_of(slot * BLOCK, BLOCK), BLOCK)
            pre = rest_in[lines, :] + t_dot(one_hot(send, slot), blocks[slot])
            sig = sigmoid(pre)
            slope[lines, :] = sig * (1.0 + pre * (1.0 - sig))
            hidden.append((pre * sig).astype(BF16))
        for i in range(GROUP):
            slot = group * GROUP + i
            mine, dz, row = mesh_place(mesh_block[slot], where)
            start = jnp.where(mine, 0, RING * HALF) + dz * HALF + row
            lines = pl.ds(pl.multiple_of(start, BLOCK), BLOCK)
            total[lines, :] += dot(one_hot(recv, slot), hidden[i])

    near[...] = total[: RING * HALF, :]
    far[...] = total[RING * HALF :, :].astype(BF16)


def pair_sum_kernel(*refs):
    near, other, outs = refs[:CHUNKS], refs[CHUNKS : 2 * CHUNKS], refs[2 * CHUNKS :]
    for chunk in range(CHUNKS):
        for step in range(RING):
            lines = pl.ds(step * HALF, HALF)
            value = near[chunk][lines, :] + other[chunk][lines, :].astype(F32)
            outs[step][:, pl.ds(chunk * COLS, COLS)] = value.astype(outs[step].dtype)


def node_kernel(cot, w_out, own, a, b, c, aggregate, grads):
    part = own[...] + (a[...].astype(F32) + b[...].astype(F32) + c[...].astype(F32))
    total = split_dot(part, w_out[...], dot)
    aggregate[...] = total
    sig = sigmoid(total)
    grad = (cot[...] * (sig * (1.0 + total * (1.0 - sig)))).astype(BF16)
    grads[...] = dot_t(grad, w_out[...]).astype(BF16)


def backward_kernel(where, live, grid_block, mesh_block, first_of, send, recv, *rest):
    slopes, pieces, outs = rest[:CHUNKS], rest[CHUNKS : CHUNKS + 8], rest[CHUNKS + 8 : -2]
    total, blocks = rest[-2:]
    for out in outs:
        out[...] = jnp.zeros_like(out)

    @pl.loop(0, live[0])
    def _(group):
        for i in range(GROUP):
            mine, dz, row = mesh_place(mesh_block[group * GROUP + i], where)
            for piece in range(8):

                @pl.when(jnp.logical_and(mine == (piece < 4), dz == piece % 4))
                def _():
                    blocks[i] = pieces[piece][pl.ds(pl.multiple_of(row, BLOCK), BLOCK), :]

        parts = []
        for i in range(GROUP):
            slot = group * GROUP + i
            lines = pl.ds(pl.multiple_of(slot * BLOCK, BLOCK), BLOCK)
            grad = t_dot(one_hot(recv, slot), blocks[i])
            grads = [(grad[:, c * COLS : (c + 1) * COLS] * slopes[c][lines, :]).astype(BF16) for c in range(CHUNKS)]
            parts.append([dot(one_hot(send, slot), g) for g in grads])
        for i in range(GROUP):
            slot = group * GROUP + i
            first = first_of[slot]
            for c in range(CHUNKS):
                cols = pl.ds(c * COLS, COLS)

                @pl.when(first == slot)
                def _():
                    total[slot, :, cols] = parts[i][c]

                @pl.when(first != slot)
                def _():
                    total[first, :, cols] += parts[i][c]

    @pl.loop(0, live[0] * GROUP)
    def _(slot):
        @pl.when(first_of[slot] == slot)
        def _():
            mine, near, far, row = grid_place(grid_block[slot], where)
            start = lax.rem(RING - near, RING) * HALF + row
            far = lax.rem(RING - far, RING)
            for c in range(CHUNKS):
                own, (give_across, give_rest) = outs[RING * c : RING * (c + 1)], outs[RING * CHUNKS :]
                for step in range(RING):

                    @pl.when(jnp.logical_and(mine, far == step))
                    def _():
                        own[step][pl.ds(pl.multiple_of(start, BLOCK), BLOCK), :] = total[slot, :, pl.ds(c * COLS, COLS)].astype(BF16)

                    @pl.when(jnp.logical_and(jnp.logical_not(mine), far == step))
                    def _():
                        to, place = (give_across, c) if step == 2 else (give_rest, 3 * c + min(step, 2))
                        place = start + place * GATHERED
                        to[pl.ds(pl.multiple_of(place, BLOCK), BLOCK), :] = total[slot, :, pl.ds(c * COLS, COLS)].astype(BF16)


def add(a, b):
    return (a[...].astype(F32) + b[...].astype(F32)).astype(BF16)


def merge_kernel(base, up, down, other, into_up, into_down, out_up, out_down):
    out_up[:GATHERED, :] = add(up, into_up)
    out_up[GATHERED:, :] = other[pl.ds(base + GATHERED, GATHERED), :]
    out_down[:GATHERED, :] = down[...]
    out_down[GATHERED:, :] = add(other.at[pl.ds(base + 2 * GATHERED, GATHERED), :], into_down)


def column_sum_kernel(base, own, other, up, down, here, *outs):
    for half, (term, first) in enumerate(((own, 0), (other, base))):
        for step in range(RING):
            both = pl.ds(half * GATHERED + step * HALF, HALF)
            value = term[pl.ds(first + step * HALF, HALF), :].astype(F32) + (up[both, :].astype(F32) + down[both, :].astype(F32))
            place = pl.ds(half * HALF, HALF)
            if step == 0:
                here[place, :] = value
            else:
                outs[step - 1][place, :] = value.astype(BF16)


def row_sum_kernel(here, up, down, across, own, other):
    value = here[...] + (up[...].astype(F32) + down[...].astype(F32) + across[...].astype(F32))
    own[...] = value[:HALF, :]
    other[...] = value[HALF:, :]


def grid_grad_kernel(where, w_grid, *rest):
    out = rest[-1]
    core = where[1]
    for which in range(2):
        value = jnp.zeros((HALF, WIDTH), F32)
        for chunk in range(CHUNKS):
            value += split_dot(rest[2 * chunk + which][...], w_grid[:, chunk * COLS : (chunk + 1) * COLS], dot_t)
        place = core if which == 0 else 1 - core
        out[pl.ds(pl.multiple_of(place * HALF, HALF), HALF), :] = value


def per_device(
    grid,
    mesh_latent,
    edge_latent,
    edge_grid_block,
    edge_mesh_block,
    sender_offset,
    receiver_offset,
    live_groups,
    w_grid,
    w_mesh,
    w_edge,
    bias,
    w_out,
    w_node,
    cotangent,
):
    where = jnp.stack([lax.axis_index(a) for a in ("z", "core", "x", "y")]).astype(jnp.int32)
    edges = SLOTS * BLOCK
    both_chunks = range(CHUNKS)

    def call(kernel, name, outs, *args, scalars=0, scratch=(), spec=VMEM):
        whole = [SMEM] * scalars + [VMEM] * (len(args) - scalars)
        if spec is ANY:
            whole[-6:] = [ANY] * 6
        return pl.pallas_call(
            kernel,
            in_specs=whole,
            out_specs=[VMEM] * len(outs),
            out_shape=outs,
            scratch_shapes=scratch,
            compiler_params=params(),
            cost_estimate=LIGHT,
            name=name,
        )(*args)

    keep, give = call(
        first_product_kernel, "first_product", [shape(HALF, WIDTH, BF16)] * 2, where, grid, w_grid, scalars=1
    )
    got = swap(give)
    mine = jnp.concatenate([keep, got], axis=0)
    mesh_pair = pair_z(after(mesh_latent, mine), 1)

    def far_gather(value):
        return shift(value, False, 1), shift(value, False, -1)

    def give_rows(both, up, down):
        return jnp.concatenate([both[GATHERED:], up[GATHERED:], down[GATHERED:]], axis=0)

    near = shift(mine, True, 1), shift(mine, True, 2), shift(mine, True, -1)
    ring_0, ring_1 = call(
        ring_kernel, "ring", [shape(2 * GATHERED, COLS, BF16)] * CHUNKS, keep, got, *after(near, mesh_pair)
    )

    mesh_near = jnp.concatenate([mesh_latent, mesh_pair], axis=0)
    mesh_far = pair_z(after(mesh_near, ring_0), 3)
    (up_0, down_0), mesh_far = lax.optimization_barrier((far_gather(ring_0), mesh_far))
    across_0 = shift(up_0[:GATHERED], False, 1), shift(down_0[GATHERED:], False, -1)
    far_1 = far_gather(after(ring_1, up_0))
    mesh_rows = jnp.concatenate([mesh_near, mesh_far], axis=0)
    mesh_pieces = [mesh_rows, swap(mesh_rows)]
    edge_terms = call(
        edge_kernel,
        "edge_terms",
        [shape(edges, COLS, F32)] * CHUNKS,
        where,
        live_groups,
        edge_mesh_block,
        receiver_offset,
        edge_latent,
        w_mesh,
        w_edge,
        bias.reshape(1, WIDTH),
        *mesh_pieces,
        scalars=3,
        scratch=[pltpu.VMEM((GROUP, BLOCK, WIDTH), BF16), pltpu.VMEM((GROUP * BLOCK, WIDTH), BF16)],
    )
    cot = dot_t(cotangent, w_node)

    got_0 = swap(after(give_rows(ring_0, up_0, down_0), mesh_pieces[1]))
    own_across, other_across = lax.optimization_barrier(across_0)
    far_got_0 = swap(after(other_across, got_0))
    (up_1, down_1), edge_terms, got_0, far_got_0 = lax.optimization_barrier((far_1, edge_terms, got_0, far_got_0))
    across_1 = shift(up_1[:GATHERED], False, 1), shift(down_1[GATHERED:], False, -1)

    def forward(chunk, own, got):
        return call(
            forward_kernel,
            f"forward_{chunk}",
            [shape(edges, COLS, F32), shape(RING * HALF, COLS, F32), shape(RING * HALF, COLS, BF16)],
            where,
            live_groups,
            edge_grid_block,
            edge_mesh_block,
            sender_offset,
            receiver_offset,
            edge_terms[chunk],
            *own,
            *got,
            scalars=4,
            scratch=[
                pltpu.VMEM((2 * RING * HALF, COLS), F32),
                pltpu.VMEM((SLOTS, BLOCK, COLS), BF16),
                pltpu.SemaphoreType.DMA((SLOTS,)),
            ],
            spec=ANY,
        )

    def pair_sum(*terms):
        outs = [shape(HALF, WIDTH, F32)] + [shape(HALF, WIDTH, BF16)] * 3
        return call(pair_sum_kernel, "pair_sum", outs, *terms)

    def band_sum(own, a, b, c):
        return [own, shift_z(a, 1), shift_z(c, -1), shift_z(b, 2)]

    slope_0, near_sum_0, far_sum_0 = forward(0, (ring_0, up_0, own_across, down_0), (got_0, far_got_0))
    got_1 = swap(give_rows(ring_1, up_1, down_1))
    (own_across, other_across), got_1, far_sum_0, cot = lax.optimization_barrier((across_1, got_1, far_sum_0, cot))
    far_got_1, far_sum_0 = swap(other_across), swap(far_sum_0)
    slope_1, near_sum_1, far_sum_1 = forward(
        1, (ring_1, up_1, own_across, down_1), (got_1, after(far_got_1, far_sum_0))
    )
    sums = band_sum(*pair_sum(near_sum_0, near_sum_1, far_sum_0, swap(far_sum_1)))
    slopes = [slope_0, slope_1]

    aggregate, grads = call(
        node_kernel, "node", [shape(HALF, WIDTH, F32), shape(HALF, WIDTH, BF16)], cot, w_out, *sums
    )

    slots = jnp.arange(SLOTS)
    same = edge_grid_block[:, None] == edge_grid_block[None, :]
    first_of = jnp.min(jnp.where(same, slots[None, :], SLOTS), axis=1).astype(jnp.int32)

    band = [grads, shift_z(grads, -1), shift_z(grads, 2), shift_z(grads, 1)]
    partial = call(
        backward_kernel,
        "backward",
        [shape(GATHERED, COLS, BF16)] * (RING * CHUNKS)
        + [shape(CHUNKS * GATHERED, COLS, BF16), shape(3 * CHUNKS * GATHERED, COLS, BF16)],
        where,
        live_groups,
        edge_grid_block,
        edge_mesh_block,
        first_of,
        sender_offset,
        receiver_offset,
        *slopes,
        *band,
        *[swap(p) for p in band],
        scalars=5,
        scratch=[pltpu.VMEM((SLOTS, BLOCK, WIDTH), F32), pltpu.VMEM((GROUP, BLOCK, WIDTH), BF16)],
    )
    own_0, own_1, give_across, give_rest = partial[:RING], partial[RING : 2 * RING], partial[-2], partial[-1]

    def merge(chunk, own, other, into):
        kernel = functools.partial(merge_kernel, 3 * chunk * GATHERED)
        return call(kernel, f"merge_{chunk}", [shape(2 * GATHERED, COLS, BF16)] * 2, own[1], own[3], other, *into)

    def column_sum(chunk, own, other, far):
        outs = [shape(2 * HALF, COLS, F32)] + [shape(2 * HALF, COLS, BF16)] * 3
        kernel = functools.partial(column_sum_kernel, 3 * chunk * GATHERED)
        return call(kernel, f"column_sum_{chunk}", outs, own[0], other, *far)

    def far_send(up, down):
        return shift(up, False, 1), shift(down, False, -1)

    def near_send(here, a, b, c):
        return here, shift(a, True, 1), shift(b, True, 2), shift(c, True, -1)

    def row_sum(chunk, terms):
        return call(row_sum_kernel, f"row_sum_{chunk}", [shape(HALF, COLS, F32)] * 2, *terms)

    across = swap(give_across)
    other = swap(after(give_rest, across))
    into_0 = shift(own_0[2], False, 1), shift(across[:GATHERED], False, -1)
    into_1 = shift(own_1[2], False, 1), shift(across[GATHERED:], False, -1)
    merged = merge(0, own_0, other, into_0)
    far_0 = far_send(*merged)
    merged = merge(1, own_1, after(other, merged), into_1)
    far_1 = far_send(*merged)
    activation = jax.nn.silu(aggregate).astype(BF16)
    mesh_out = (mesh_latent.astype(F32) + dot(activation, w_node)).astype(BF16)
    columns = column_sum(0, own_0, other, after(far_0, merged, mesh_out))
    rows_0 = near_send(*columns)
    columns = column_sum(1, own_1, other, after(far_1, columns))
    rows_1 = near_send(*columns)
    mine_0, give_0 = row_sum(0, after(rows_0, columns))
    got_0 = swap(give_0)
    mine_1, give_1 = row_sum(1, after(rows_1, give_0))
    parts = [mine_0, got_0, mine_1, swap(give_1)]

    grid_grad = call(
        grid_grad_kernel, "grid_grad", [shape(2 * HALF, WIDTH, F32)], where, w_grid, *parts, scalars=1
    )[0]
    return (mesh_out, grid_grad)


def solution(mesh):
    split = Mesh(mesh.devices.reshape(4, 2, 4, 4), ("z", "core", "x", "y"))
    rows = P(("z", "core", "x", "y"))
    placed = (rows,) * 8 + (P(),) * 6 + (rows,)
    return jax.shard_map(per_device, mesh=split, in_specs=placed, out_specs=(rows, rows), check_vma=False)
```

```python
import functools

import jax
import jax.numpy as jnp
from jax import lax
from jax.experimental import pallas as pl
from jax.experimental.pallas import tpu as pltpu
from jax.sharding import Mesh
from jax.sharding import PartitionSpec as P

F32 = jnp.float32
BF16 = jnp.bfloat16
RING = 4
BLOCK = 128
SLOTS = 16
GROUP = 4
WIDTH = 512
CHUNKS = 2
COLS = WIDTH // CHUNKS
HALF = 256
GATHERED = RING * HALF
VMEM = pl.BlockSpec(memory_space=pltpu.VMEM)
SMEM = pl.BlockSpec(memory_space=pltpu.SMEM)
ANY = pl.BlockSpec(memory_space=pl.ANY)
LIGHT = pl.CostEstimate(flops=0, bytes_accessed=0, transcendentals=0)
LIMIT = 20 * 1024 * 1024


def shape(rows, cols, dtype):
    return jax.ShapeDtypeStruct((rows, cols), dtype)


def params():
    return pltpu.CompilerParams(vmem_limit_bytes=LIMIT)


CHIP_AXES = ("core", "x", "y")


def along(first, step):
    pairs = []
    for core in range(2):
        for x in range(RING):
            for y in range(RING):
                if (core == 0) == first:
                    to = ((x + step) % RING, y)
                else:
                    to = (x, (y + step) % RING)
                pairs.append((core * 16 + x * RING + y, core * 16 + to[0] * RING + to[1]))
    return pairs


def shift(value, first, step):
    return lax.ppermute(value, CHIP_AXES, along(first, step))


def shift_z(value, step):
    return lax.ppermute(value, "z", [(i, (i + step) % RING) for i in range(RING)])


def after(value, *others):
    return lax.optimization_barrier((value, others))[0]


def pair_z(value, flip):
    return lax.ppermute(value, "z", [(i, i ^ flip) for i in range(RING)])


def swap(value):
    return lax.ppermute(value, "core", [(0, 1), (1, 0)])


def dot(a, b):
    return jnp.dot(a, b, preferred_element_type=F32)


def dot_t(a, b):
    return lax.dot_general(a, b, (((1,), (1,)), ((), ())), preferred_element_type=F32)


def split_dot(a, b, product):
    high = a.astype(BF16)
    low = (a - high.astype(F32)).astype(BF16)
    return product(high, b) + product(low, b)


def sigmoid(value):
    return 1.0 / (1.0 + jnp.exp(-value))


def one_hot(offsets, slot):
    rows = lax.broadcasted_iota(jnp.int32, (BLOCK, BLOCK), 0)
    return (rows == offsets[pl.ds(slot, 1), :]).astype(BF16)


def grid_place(block, where):
    core, x, y = where[1], where[2], where[3]
    owner = block // 4
    kind = (block % 4) // 2
    dx = lax.rem(x - owner // 4 + RING, RING)
    dy = lax.rem(y - owner % 4 + RING, RING)
    mine = kind == core
    near = jnp.where(kind == 0, dx, dy)
    far = jnp.where(kind == 0, dy, dx)
    return mine, near, far, (block % 2) * BLOCK


def mesh_place(block, where):
    owner = block // 2
    dz = lax.rem(owner // 2 - where[0] + RING, RING)
    return owner % 2 == where[1], dz, (block % 2) * BLOCK


def first_product_kernel(where, grid, w_grid, keep, give):
    core = where[1]
    for out, half in ((give, 1 - core), (keep, core)):
        out[...] = dot(grid[pl.ds(pl.multiple_of(half * HALF, HALF), HALF), :], w_grid[...]).astype(BF16)


def ring_kernel(keep, got, up, across, down, *outs):
    for chunk, out in enumerate(outs):
        cols = pl.ds(chunk * COLS, COLS)
        out[:HALF, :] = keep[:, cols]
        out[GATHERED : GATHERED + HALF, :] = got[:, cols]
        for step, term in enumerate((up, across, down)):
            out[pl.ds((step + 1) * HALF, HALF), :] = term[:HALF, cols]
            out[pl.ds(GATHERED + (step + 1) * HALF, HALF), :] = term[HALF:, cols]


def edge_kernel(where, live, mesh_block, pick, edge, w_mesh, w_edge, bias, *rest):
    pieces, outs, (blocks, rows) = rest[:2], rest[2 : 2 + CHUNKS], rest[-2:]

    @pl.loop(0, live[0])
    def _(group):
        for i in range(GROUP):
            block = mesh_block[group * GROUP + i]
            owner = block // 2
            flip = (owner // 2) ^ where[0]
            mine = owner % 2 == where[1]
            row = flip * HALF + (block % 2) * BLOCK

            @pl.when(mine)
            def _():
                blocks[i] = pieces[0][pl.ds(pl.multiple_of(row, BLOCK), BLOCK), :]

            @pl.when(jnp.logical_not(mine))
            def _():
                for chunk in range(CHUNKS):
                    lines = pl.ds(pl.multiple_of((3 + chunk) * GATHERED + row, BLOCK), BLOCK)
                    blocks[i, :, pl.ds(chunk * COLS, COLS)] = pieces[1][lines, :]

        first = group * GROUP * BLOCK
        for i in range(GROUP):
            at = pl.ds(pl.multiple_of(first + i * BLOCK, BLOCK), BLOCK)
            rows[pl.ds(i * BLOCK, BLOCK), :] = dot(pick[at, :], blocks[i]).astype(BF16)
        lines = pl.ds(pl.multiple_of(first, GROUP * BLOCK), GROUP * BLOCK)
        for chunk in range(CHUNKS):
            cols = pl.ds(chunk * COLS, COLS)
            outs[chunk][lines, :] = dot(rows[...], w_mesh[:, cols]) + dot(edge[lines, :], w_edge[:, cols]) + bias[:, cols]


def forward_kernel(where, live, grid_block, mesh_block, pick, recv, rest_in, *rest):
    pieces, (slope, near, far) = rest[:6], rest[6:9]
    total, blocks, sems = rest[9:]

    @pl.loop(0, live[0] * GROUP)
    def _(slot):
        mine, first, second, row = grid_place(grid_block[slot], where)
        start = first * HALF + row

        def fetch(piece, base):
            lines = pl.ds(pl.multiple_of(base + start, BLOCK), BLOCK)
            pltpu.make_async_copy(pieces[piece].at[lines, :], blocks.at[slot], sems.at[slot]).start()

        for piece in range(RING):

            @pl.when(jnp.logical_and(mine, second == piece))
            def _():
                fetch(piece, 0)

        @pl.when(jnp.logical_and(jnp.logical_not(mine), second != 2))
        def _():
            fetch(RING, jnp.minimum(second, 2) * GATHERED)

        @pl.when(jnp.logical_and(jnp.logical_not(mine), second == 2))
        def _():
            fetch(RING + 1, 0)

    total[...] = jnp.zeros_like(total)

    @pl.loop(0, live[0])
    def _(group):
        slots = [group * GROUP + i for i in range(GROUP)]
        for slot in slots:
            pltpu.make_async_copy(pieces[0].at[pl.ds(0, BLOCK), :], blocks.at[slot], sems.at[slot]).wait()
        lines = [pl.ds(pl.multiple_of(slot * BLOCK, BLOCK), BLOCK) for slot in slots]
        pres = [rest_in[at, :] + dot(pick[at, :], blocks[slot]) for at, slot in zip(lines, slots)]
        sigs = [sigmoid(pre) for pre in pres]
        for at, pre, sig in zip(lines, pres, sigs):
            slope[at, :] = sig * (1.0 + pre * (1.0 - sig))
        sums = [dot(one_hot(recv, slot), (pre * sig).astype(BF16)) for slot, pre, sig in zip(slots, pres, sigs)]
        for slot, value in zip(slots, sums):
            mine, dz, row = mesh_place(mesh_block[slot], where)
            start = jnp.where(mine, 0, RING * HALF) + dz * HALF + row
            total[pl.ds(pl.multiple_of(start, BLOCK), BLOCK), :] += value

    near[...] = total[: RING * HALF, :]
    far[...] = total[RING * HALF :, :].astype(BF16)


def pair_sum_kernel(*refs):
    near, other, outs = refs[:CHUNKS], refs[CHUNKS : 2 * CHUNKS], refs[2 * CHUNKS :]
    for chunk in range(CHUNKS):
        for step in range(RING):
            lines = pl.ds(step * HALF, HALF)
            value = near[chunk][lines, :] + other[chunk][lines, :].astype(F32)
            outs[step][:, pl.ds(chunk * COLS, COLS)] = value.astype(outs[step].dtype)


def node_kernel(cot, w_out, own, a, b, c, aggregate, grads):
    part = own[...] + (a[...].astype(F32) + b[...].astype(F32) + c[...].astype(F32))
    total = split_dot(part, w_out[...], dot)
    aggregate[...] = total
    sig = sigmoid(total)
    grad = (cot[...] * (sig * (1.0 + total * (1.0 - sig)))).astype(BF16)
    grads[...] = dot_t(grad, w_out[...]).astype(BF16)


def backward_kernel(where, live, grid_block, mesh_block, first_of, pick, send, *rest):
    slopes, pieces, outs = rest[:CHUNKS], rest[CHUNKS : CHUNKS + 8], rest[CHUNKS + 8 : -2]
    total, blocks = rest[-2:]
    for out in outs:
        out[...] = jnp.zeros_like(out)

    @pl.loop(0, live[0])
    def _(group):
        slots = [group * GROUP + i for i in range(GROUP)]
        for i, slot in enumerate(slots):
            mine, dz, row = mesh_place(mesh_block[slot], where)
            at = jnp.where(mine, dz, dz + RING)
            for piece in range(8):

                @pl.when(at == piece)
                def _():
                    blocks[i] = pieces[piece][pl.ds(pl.multiple_of(row, BLOCK), BLOCK), :]

        lines = [pl.ds(pl.multiple_of(slot * BLOCK, BLOCK), BLOCK) for slot in slots]
        hot = [one_hot(send, slot) for slot in slots]
        for c in range(CHUNKS):
            cols = pl.ds(c * COLS, COLS)
            grads = [dot(pick[at, :], blocks[i, :, cols]) * slopes[c][at, :] for i, at in enumerate(lines)]
            parts = [dot(hot[i], grad.astype(BF16)) for i, grad in enumerate(grads)]
            for slot, part in zip(slots, parts):
                first = first_of[slot]
                total[first, :, cols] = jnp.where(first == slot, 0.0, total[first, :, cols]) + part

    @pl.loop(0, live[0] * GROUP)
    def _(slot):
        mine, near, far, row = grid_place(grid_block[slot], where)
        start = lax.rem(RING - near, RING) * HALF + row
        far = lax.rem(RING - far, RING)
        at = jnp.where(first_of[slot] == slot, jnp.where(mine, far, jnp.where(far == 2, RING, RING + 1)), -1)
        for step in range(RING + 2):

            @pl.when(at == step)
            def _():
                for c in range(CHUNKS):
                    if step < RING:
                        to, place = outs[RING * c + step], start
                    elif step == RING:
                        to, place = outs[-2], start + c * GATHERED
                    else:
                        to, place = outs[-1], start + (3 * c + jnp.minimum(far, 2)) * GATHERED
                    to[pl.ds(pl.multiple_of(place, BLOCK), BLOCK), :] = total[slot, :, pl.ds(c * COLS, COLS)].astype(BF16)


def add(a, b):
    return (a[...].astype(F32) + b[...].astype(F32)).astype(BF16)


def merge_kernel(terms, *refs):
    into_up, into_down, out_up, out_down = refs[-4:]
    up_0, up_1, down_0, down_1 = [refs[i].at[pl.ds(base, GATHERED), :] for i, base in terms]
    out_up[:GATHERED, :] = add(up_0, into_up)
    out_up[GATHERED:, :] = up_1[...]
    out_down[:GATHERED, :] = down_0[...]
    out_down[GATHERED:, :] = add(down_1, into_down)


def column_sum_kernel(terms, *refs):
    up, down, here, *outs = refs[-6:]
    for chunk, (i, base) in enumerate(terms):
        cols = pl.ds(chunk * COLS, COLS)
        for step in range(RING):
            both = pl.ds(chunk * GATHERED + step * HALF, HALF)
            value = refs[i][pl.ds(base + step * HALF, HALF), :].astype(F32) + (up[both, :].astype(F32) + down[both, :].astype(F32))
            if step == 0:
                here[:, cols] = value
            else:
                outs[step - 1][:, cols] = value.astype(BF16)


def row_sum_kernel(w_grid, here, up, down, across, out):
    value = here[...] + (up[...].astype(F32) + down[...].astype(F32) + across[...].astype(F32))
    out[...] = split_dot(value, w_grid[...], dot_t)


def place_kernel(other, where, value, *rest):
    out, sem = rest[-2:]
    place = 1 - where[1] if other else where[1]
    copy = pltpu.make_async_copy(value, out.at[pl.ds(pl.multiple_of(place * HALF, HALF), HALF), :], sem)
    copy.start()
    copy.wait()


def per_device(
    grid,
    mesh_latent,
    edge_latent,
    edge_grid_block,
    edge_mesh_block,
    sender_offset,
    receiver_offset,
    live_groups,
    w_grid,
    w_mesh,
    w_edge,
    bias,
    w_out,
    w_node,
    cotangent,
):
    def picks(offsets):
        return (offsets.reshape(-1, 1) == jnp.arange(BLOCK, dtype=jnp.int32)).astype(BF16)

    pick_send, pick_recv = picks(sender_offset), picks(receiver_offset)
    where = jnp.stack([lax.axis_index(a) for a in ("z", "core", "x", "y")]).astype(jnp.int32)
    edges = SLOTS * BLOCK
    both_chunks = range(CHUNKS)

    def call(kernel, name, outs, *args, scalars=0, scratch=(), spec=VMEM):
        whole = [SMEM] * scalars + [VMEM] * (len(args) - scalars)
        if spec is ANY:
            whole[-6:] = [ANY] * 6
        return pl.pallas_call(
            kernel,
            in_specs=whole,
            out_specs=[VMEM] * len(outs),
            out_shape=outs,
            scratch_shapes=scratch,
            compiler_params=params(),
            cost_estimate=LIGHT,
            name=name,
        )(*args)

    keep, give = call(
        first_product_kernel, "first_product", [shape(HALF, WIDTH, BF16)] * 2, where, grid, w_grid, scalars=1
    )
    got = swap(give)
    mine = jnp.concatenate([keep, got], axis=0)
    mesh_first = after(mesh_latent, mine)
    mesh_pair = pair_z(mesh_first, 1), pair_z(mesh_first, 3)

    def far_gather(value):
        return shift(value, False, 1), shift(value, False, -1)

    def give_rows(both, up, down):
        return jnp.concatenate([both[GATHERED:], up[GATHERED:], down[GATHERED:]], axis=0)

    near = shift(mine, True, 1), shift(mine, True, 2), shift(mine, True, -1)
    ring_0, ring_1 = call(
        ring_kernel, "ring", [shape(2 * GATHERED, COLS, BF16)] * CHUNKS, keep, got, *after(near, mesh_pair)
    )

    mesh_far = pair_z(after(mesh_pair[1], ring_0), 1)
    (up_0, down_0), mesh_far = lax.optimization_barrier((far_gather(ring_0), mesh_far))
    mesh_rows = jnp.concatenate([mesh_latent, mesh_pair[0], mesh_far, mesh_pair[1]], axis=0)
    give = [give_rows(ring_0, up_0, down_0)] + [mesh_rows[:, c * COLS : (c + 1) * COLS] for c in both_chunks]
    got_0 = swap(jnp.concatenate(give, axis=0))
    across_0 = shift(up_0[:GATHERED], False, 1), shift(down_0[GATHERED:], False, -1)
    far_1 = far_gather(after(ring_1, up_0))
    edge_terms = call(
        edge_kernel,
        "edge_terms",
        [shape(edges, COLS, F32)] * CHUNKS,
        where,
        live_groups,
        edge_mesh_block,
        pick_recv,
        edge_latent,
        w_mesh,
        w_edge,
        bias.reshape(1, WIDTH),
        mesh_rows,
        got_0,
        scalars=3,
        scratch=[pltpu.VMEM((GROUP, BLOCK, WIDTH), BF16), pltpu.VMEM((GROUP * BLOCK, WIDTH), BF16)],
    )
    cot = dot_t(cotangent, w_node)

    own_across, other_across = lax.optimization_barrier(across_0)
    far_got_0 = swap(other_across)
    (up_1, down_1), edge_terms, got_0, far_got_0 = lax.optimization_barrier((far_1, edge_terms, got_0, far_got_0))
    across_1 = shift(up_1[:GATHERED], False, 1), shift(down_1[GATHERED:], False, -1)

    def forward(chunk, own, got):
        return call(
            forward_kernel,
            f"forward_{chunk}",
            [shape(edges, COLS, F32), shape(RING * HALF, COLS, F32), shape(RING * HALF, COLS, BF16)],
            where,
            live_groups,
            edge_grid_block,
            edge_mesh_block,
            pick_send,
            receiver_offset,
            edge_terms[chunk],
            *own,
            *got,
            scalars=4,
            scratch=[
                pltpu.VMEM((2 * RING * HALF, COLS), F32),
                pltpu.VMEM((SLOTS, BLOCK, COLS), BF16),
                pltpu.SemaphoreType.DMA((SLOTS,)),
            ],
            spec=ANY,
        )

    def pair_sum(*terms):
        outs = [shape(HALF, WIDTH, F32)] + [shape(HALF, WIDTH, BF16)] * 3
        return call(pair_sum_kernel, "pair_sum", outs, *terms)

    def band_sum(own, a, b, c):
        return [own, shift_z(a, 1), shift_z(c, -1), shift_z(b, 2)]

    slope_0, near_sum_0, far_sum_0 = forward(0, (ring_0, up_0, own_across, down_0), (got_0, far_got_0))
    got_1 = swap(give_rows(ring_1, up_1, down_1))
    (own_across, other_across), got_1, far_sum_0, cot = lax.optimization_barrier((across_1, got_1, far_sum_0, cot))
    far_got_1, far_sum_0 = swap(other_across), swap(far_sum_0)
    slope_1, near_sum_1, far_sum_1 = forward(
        1, (ring_1, up_1, own_across, down_1), (got_1, after(far_got_1, far_sum_0))
    )
    sums = band_sum(*pair_sum(near_sum_0, near_sum_1, far_sum_0, swap(far_sum_1)))
    slopes = [slope_0, slope_1]

    aggregate, grads = call(
        node_kernel, "node", [shape(HALF, WIDTH, F32), shape(HALF, WIDTH, BF16)], cot, w_out, *sums
    )

    slots = jnp.arange(SLOTS)
    same = edge_grid_block[:, None] == edge_grid_block[None, :]
    first_of = jnp.min(jnp.where(same, slots[None, :], SLOTS), axis=1).astype(jnp.int32)

    band = [grads, shift_z(grads, -1), shift_z(grads, 2), shift_z(grads, 1)]
    partial = call(
        backward_kernel,
        "backward",
        [shape(GATHERED, COLS, BF16)] * (RING * CHUNKS)
        + [shape(CHUNKS * GATHERED, COLS, BF16), shape(3 * CHUNKS * GATHERED, COLS, BF16)],
        where,
        live_groups,
        edge_grid_block,
        edge_mesh_block,
        first_of,
        pick_recv,
        sender_offset,
        *slopes,
        *band,
        *[swap(p) for p in band],
        scalars=5,
        scratch=[pltpu.VMEM((SLOTS, BLOCK, WIDTH), F32), pltpu.VMEM((GROUP, BLOCK, WIDTH), BF16)],
    )
    own_0, own_1, give_across, give_rest = partial[:RING], partial[RING : 2 * RING], partial[-2], partial[-1]

    def far_send(into, name, terms, *refs):
        kernel = functools.partial(merge_kernel, terms)
        up, down = call(kernel, name, [shape(2 * GATHERED, COLS, BF16)] * 2, *refs, *into)
        return (shift(up, False, 1), shift(down, False, -1)), up

    def column_sum(far, name, terms, *refs):
        kernel = functools.partial(column_sum_kernel, terms)
        outs = [shape(HALF, WIDTH, F32)] + [shape(HALF, WIDTH, BF16)] * 3
        return call(kernel, name, outs, *refs, *far)

    def near_send(here, a, b, c):
        return here, shift(a, True, 1), shift(b, True, 2), shift(c, True, -1)

    def row_sum(name, terms):
        return call(row_sum_kernel, name, [shape(HALF, WIDTH, F32)], w_grid, *terms)[0]

    into_mine = shift(own_0[2], False, 1), shift(own_1[2], False, -1)
    across = swap(give_across)
    rest = swap(after(give_rest, across))
    into_other = shift(across[:GATHERED], False, 1), shift(across[GATHERED:], False, -1)
    far_mine, merged = far_send(
        into_mine, "merge_mine", ((0, 0), (1, 0), (2, 0), (3, 0)), own_0[1], own_1[1], own_0[3], own_1[3]
    )
    step = GATHERED
    far_other, merged = far_send(
        into_other, "merge_other", ((0, step), (0, 4 * step), (0, 2 * step), (0, 5 * step)), after(rest, merged)
    )
    activation = jax.nn.silu(aggregate).astype(BF16)
    mesh_out = (mesh_latent.astype(F32) + dot(activation, w_node)).astype(BF16)
    columns = column_sum(after(far_mine, (mesh_out, merged)), "column_sum_mine", ((0, 0), (1, 0)), own_0[0], own_1[0])
    near_mine = near_send(*columns)
    columns = column_sum(after(far_other, columns), "column_sum_other", ((0, 0), (0, 3 * step)), rest)
    near_other = near_send(*columns)
    mine = row_sum("row_sum_mine", after(near_mine, columns))

    def place(name, other, value, *into):
        return pl.pallas_call(
            functools.partial(place_kernel, other),
            in_specs=[SMEM, VMEM] + [ANY] * len(into),
            out_specs=ANY,
            out_shape=shape(2 * HALF, WIDTH, F32),
            input_output_aliases={2: 0} if into else {},
            scratch_shapes=[pltpu.SemaphoreType.DMA],
            compiler_params=params(),
            cost_estimate=LIGHT,
            name=name,
        )(where, value, *into)

    half_done = place("place_mine", False, mine)
    other = row_sum("row_sum_other", after(near_other, half_done))
    grid_grad = place("place_other", True, swap(other), half_done)
    return (mesh_out, grid_grad)


def solution(mesh):
    split = Mesh(mesh.devices.reshape(4, 2, 4, 4), ("z", "core", "x", "y"))
    rows = P(("z", "core", "x", "y"))
    placed = (rows,) * 8 + (P(),) * 6 + (rows,)
    return jax.shard_map(per_device, mesh=split, in_specs=placed, out_specs=(rows, rows), check_vma=False)
```

```python
import functools

import jax
import jax.numpy as jnp
from jax import lax
from jax.experimental import pallas as pl
from jax.experimental.pallas import tpu as pltpu
from jax.sharding import Mesh
from jax.sharding import PartitionSpec as P

F32 = jnp.float32
BF16 = jnp.bfloat16
RING = 4
BLOCK = 128
SLOTS = 16
GROUP = 4
WIDTH = 512
CHUNKS = 2
COLS = WIDTH // CHUNKS
HALF = 256
GATHERED = RING * HALF
VMEM = pl.BlockSpec(memory_space=pltpu.VMEM)
SMEM = pl.BlockSpec(memory_space=pltpu.SMEM)
ANY = pl.BlockSpec(memory_space=pl.ANY)
LIGHT = pl.CostEstimate(flops=0, bytes_accessed=0, transcendentals=0)
LIMIT = 20 * 1024 * 1024


def shape(rows, cols, dtype):
    return jax.ShapeDtypeStruct((rows, cols), dtype)


def params():
    return pltpu.CompilerParams(vmem_limit_bytes=LIMIT)


CHIP_AXES = ("core", "x", "y")


def along(first, step):
    pairs = []
    for core in range(2):
        for x in range(RING):
            for y in range(RING):
                if (core == 0) == first:
                    to = ((x + step) % RING, y)
                else:
                    to = (x, (y + step) % RING)
                pairs.append((core * 16 + x * RING + y, core * 16 + to[0] * RING + to[1]))
    return pairs


def shift(value, first, step):
    return lax.ppermute(value, CHIP_AXES, along(first, step))


def shift_z(value, step):
    return lax.ppermute(value, "z", [(i, (i + step) % RING) for i in range(RING)])


def after(value, *others):
    return lax.optimization_barrier((value, others))[0]


def pair_z(value, flip):
    return lax.ppermute(value, "z", [(i, i ^ flip) for i in range(RING)])


def swap(value):
    return lax.ppermute(value, "core", [(0, 1), (1, 0)])


def dot(a, b):
    return jnp.dot(a, b, preferred_element_type=F32)


def dot_t(a, b):
    return lax.dot_general(a, b, (((1,), (1,)), ((), ())), preferred_element_type=F32)


def split_dot(a, b, product):
    high = a.astype(BF16)
    low = (a - high.astype(F32)).astype(BF16)
    return product(high, b) + product(low, b)


def sigmoid(value):
    return 0.5 * jnp.tanh(0.5 * value) + 0.5


def one_hot(offsets, slot):
    rows = lax.broadcasted_iota(jnp.int32, (BLOCK, BLOCK), 0)
    return (rows == offsets[pl.ds(slot, 1), :]).astype(BF16)


def grid_place(block, where):
    core, x, y = where[1], where[2], where[3]
    owner = block // 4
    kind = (block % 4) // 2
    dx = lax.rem(x - owner // 4 + RING, RING)
    dy = lax.rem(y - owner % 4 + RING, RING)
    mine = kind == core
    near = jnp.where(kind == 0, dx, dy)
    far = jnp.where(kind == 0, dy, dx)
    return mine, near, far, (block % 2) * BLOCK


def mesh_place(block, where):
    owner = block // 2
    dz = lax.rem(owner // 2 - where[0] + RING, RING)
    return owner % 2 == where[1], dz, (block % 2) * BLOCK


def first_product_kernel(where, grid, w_grid, keep, give):
    core = where[1]
    for out, half in ((give, 1 - core), (keep, core)):
        out[...] = dot(grid[pl.ds(pl.multiple_of(half * HALF, HALF), HALF), :], w_grid[...]).astype(BF16)


def ring_kernel(keep, got, down, across, up, *outs):
    for chunk, out in enumerate(outs):
        cols = pl.ds(chunk * COLS, COLS)
        out[:HALF, :] = keep[:, cols]
        out[GATHERED : GATHERED + HALF, :] = got[:, cols]
        for step, term in enumerate((up, across, down)):
            out[pl.ds((step + 1) * HALF, HALF), :] = term[:HALF, cols]
            out[pl.ds(GATHERED + (step + 1) * HALF, HALF), :] = term[HALF:, cols]


def edge_kernel(where, live, mesh_block, pick, edge, w_mesh, w_edge, bias, *rest):
    pieces, outs, (blocks, rows) = rest[:2], rest[2 : 2 + CHUNKS], rest[-2:]

    @pl.loop(0, live[0])
    def _(group):
        for i in range(GROUP):
            block = mesh_block[group * GROUP + i]
            owner = block // 2
            flip = (owner // 2) ^ where[0]
            mine = owner % 2 == where[1]
            row = flip * HALF + (block % 2) * BLOCK

            @pl.when(mine)
            def _():
                blocks[i] = pieces[0][pl.ds(pl.multiple_of(row, BLOCK), BLOCK), :]

            @pl.when(jnp.logical_not(mine))
            def _():
                for chunk in range(CHUNKS):
                    lines = pl.ds(pl.multiple_of((3 + chunk) * GATHERED + row, BLOCK), BLOCK)
                    blocks[i, :, pl.ds(chunk * COLS, COLS)] = pieces[1][lines, :]

        first = group * GROUP * BLOCK
        for i in range(GROUP):
            at = pl.ds(pl.multiple_of(first + i * BLOCK, BLOCK), BLOCK)
            rows[pl.ds(i * BLOCK, BLOCK), :] = dot(pick[at, :], blocks[i]).astype(BF16)
        lines = pl.ds(pl.multiple_of(first, GROUP * BLOCK), GROUP * BLOCK)
        for chunk in range(CHUNKS):
            cols = pl.ds(chunk * COLS, COLS)
            outs[chunk][lines, :] = dot(rows[...], w_mesh[:, cols]) + dot(edge[lines, :], w_edge[:, cols]) + bias[:, cols]


def forward_kernel(where, live, grid_block, mesh_block, pick, recv, rest_in, *rest):
    pieces, (slope, near, far) = rest[:6], rest[6:9]
    total, blocks, sems = rest[9:]

    @pl.loop(0, live[0] * GROUP)
    def _(slot):
        mine, first, second, row = grid_place(grid_block[slot], where)
        start = first * HALF + row

        def fetch(piece, base):
            lines = pl.ds(pl.multiple_of(base + start, BLOCK), BLOCK)
            pltpu.make_async_copy(pieces[piece].at[lines, :], blocks.at[slot], sems.at[slot]).start()

        for piece in range(RING):

            @pl.when(jnp.logical_and(mine, second == piece))
            def _():
                fetch(piece, 0)

        @pl.when(jnp.logical_and(jnp.logical_not(mine), second != 2))
        def _():
            fetch(RING, jnp.minimum(second, 2) * GATHERED)

        @pl.when(jnp.logical_and(jnp.logical_not(mine), second == 2))
        def _():
            fetch(RING + 1, 0)

    total[...] = jnp.zeros_like(total)

    @pl.loop(0, live[0])
    def _(group):
        slots = [group * GROUP + i for i in range(GROUP)]
        for slot in slots:
            pltpu.make_async_copy(pieces[0].at[pl.ds(0, BLOCK), :], blocks.at[slot], sems.at[slot]).wait()
        for slot in slots:
            at = pl.ds(pl.multiple_of(slot * BLOCK, BLOCK), BLOCK)
            pre = rest_in[at, :] + dot(pick[at, :], blocks[slot])
            sig = sigmoid(pre)
            slope[at, :] = sig * (1.0 + pre * (1.0 - sig))
            value = dot(one_hot(recv, slot), (pre * sig).astype(BF16))
            mine, dz, row = mesh_place(mesh_block[slot], where)
            start = jnp.where(mine, 0, RING * HALF) + dz * HALF + row
            total[pl.ds(pl.multiple_of(start, BLOCK), BLOCK), :] += value

    near[...] = total[: RING * HALF, :]
    far[...] = total[RING * HALF :, :].astype(BF16)


def pair_sum_kernel(*refs):
    near, other, outs = refs[:CHUNKS], refs[CHUNKS : 2 * CHUNKS], refs[2 * CHUNKS :]
    for chunk in range(CHUNKS):
        for step in range(RING):
            lines = pl.ds(step * HALF, HALF)
            value = near[chunk][lines, :] + other[chunk][lines, :].astype(F32)
            outs[step][:, pl.ds(chunk * COLS, COLS)] = value.astype(outs[step].dtype)


def node_kernel(cot, w_out, own, a, b, c, aggregate, grads):
    part = own[...] + (a[...].astype(F32) + b[...].astype(F32) + c[...].astype(F32))
    total = split_dot(part, w_out[...], dot)
    aggregate[...] = total
    sig = sigmoid(total)
    grad = (cot[...] * (sig * (1.0 + total * (1.0 - sig)))).astype(BF16)
    grads[...] = dot_t(grad, w_out[...]).astype(BF16)


def zeros_kernel(*outs):
    for out in outs:
        out[...] = jnp.zeros_like(out)


def backward_kernel(where, live, grid_block, mesh_block, first_of, pick, send, *rest):
    slopes, pieces = rest[:CHUNKS], rest[CHUNKS : CHUNKS + 8]
    outs, (total, blocks) = rest[-2 - RING * CHUNKS - 2 : -2], rest[-2:]

    @pl.loop(0, live[0])
    def _(group):
        slots = [group * GROUP + i for i in range(GROUP)]
        for i, slot in enumerate(slots):
            mine, dz, row = mesh_place(mesh_block[slot], where)
            at = jnp.where(mine, dz, dz + RING)
            for piece in range(8):

                @pl.when(at == piece)
                def _():
                    blocks[i] = pieces[piece][pl.ds(pl.multiple_of(row, BLOCK), BLOCK), :]

        for i, slot in enumerate(slots):
            at = pl.ds(pl.multiple_of(slot * BLOCK, BLOCK), BLOCK)
            hot = one_hot(send, slot)
            first = first_of[slot]
            for c in range(CHUNKS):
                cols = pl.ds(c * COLS, COLS)
                grad = dot(pick[at, :], blocks[i, :, cols]) * slopes[c][at, :]
                part = dot(hot, grad.astype(BF16))
                total[first, :, cols] = jnp.where(first == slot, 0.0, total[first, :, cols]) + part

    @pl.loop(0, live[0] * GROUP)
    def _(slot):
        mine, near, far, row = grid_place(grid_block[slot], where)
        start = lax.rem(RING - near, RING) * HALF + row
        far = lax.rem(RING - far, RING)
        at = jnp.where(first_of[slot] == slot, jnp.where(mine, far, jnp.where(far == 2, RING, RING + 1)), -1)
        for step in range(RING + 2):

            @pl.when(at == step)
            def _():
                for c in range(CHUNKS):
                    if step < RING:
                        to, place = outs[RING * c + step], start
                    elif step == RING:
                        to, place = outs[-2], start + c * GATHERED
                    else:
                        to, place = outs[-1], start + (3 * c + jnp.minimum(far, 2)) * GATHERED
                    to[pl.ds(pl.multiple_of(place, BLOCK), BLOCK), :] = total[slot, :, pl.ds(c * COLS, COLS)].astype(BF16)


def add(a, b):
    return (a[...].astype(F32) + b[...].astype(F32)).astype(BF16)


def merge_kernel(terms, *refs):
    into_up, into_down, out_up, out_down = refs[-4:]
    up_0, up_1, down_0, down_1 = [refs[i].at[pl.ds(base, GATHERED), :] for i, base in terms]
    out_up[:GATHERED, :] = add(up_0, into_up)
    out_up[GATHERED:, :] = up_1[...]
    out_down[:GATHERED, :] = down_0[...]
    out_down[GATHERED:, :] = add(down_1, into_down)


def column_sum_kernel(terms, *refs):
    up, down, here, *outs = refs[-6:]
    for chunk, (i, base) in enumerate(terms):
        cols = pl.ds(chunk * COLS, COLS)
        for step in range(RING):
            both = pl.ds(chunk * GATHERED + step * HALF, HALF)
            value = refs[i][pl.ds(base + step * HALF, HALF), :].astype(F32) + (up[both, :].astype(F32) + down[both, :].astype(F32))
            if step == 0:
                here[:, cols] = value
            else:
                outs[step - 1][:, cols] = value.astype(BF16)


def row_sum_kernel(w_grid, here, up, down, across, out):
    value = here[...] + (up[...].astype(F32) + down[...].astype(F32) + across[...].astype(F32))
    out[...] = split_dot(value, w_grid[...], dot_t)


def place(row, value, out, sem):
    copy = pltpu.make_async_copy(value, out.at[pl.ds(pl.multiple_of(row, HALF), HALF), :], sem)
    copy.start()
    copy.wait()


def place_other_kernel(where, value, out, sem):
    place((1 - where[1]) * HALF, value, out, sem)


def place_mine_kernel(where, w_grid, here, up, down, across, placed, out, value, sem):
    row_sum_kernel(w_grid, here, up, down, across, value)
    place(where[1] * HALF, value, out, sem)


def per_device(
    grid,
    mesh_latent,
    edge_latent,
    edge_grid_block,
    edge_mesh_block,
    sender_offset,
    receiver_offset,
    live_groups,
    w_grid,
    w_mesh,
    w_edge,
    bias,
    w_out,
    w_node,
    cotangent,
):
    def picks(offsets):
        return (offsets.reshape(-1, 1) == jnp.arange(BLOCK, dtype=jnp.int32)).astype(BF16)

    pick_send, pick_recv = picks(sender_offset), picks(receiver_offset)
    where = jnp.stack([lax.axis_index(a) for a in ("z", "core", "x", "y")]).astype(jnp.int32)
    edges = SLOTS * BLOCK
    both_chunks = range(CHUNKS)

    def call(kernel, name, outs, *args, scalars=0, scratch=(), spec=VMEM):
        whole = [SMEM] * scalars + [VMEM] * (len(args) - scalars)
        if spec is ANY:
            whole[-6:] = [ANY] * 6
        return pl.pallas_call(
            kernel,
            in_specs=whole,
            out_specs=[VMEM] * len(outs),
            out_shape=outs,
            scratch_shapes=scratch,
            compiler_params=params(),
            cost_estimate=LIGHT,
            name=name,
        )(*args)

    keep, give = call(
        first_product_kernel, "first_product", [shape(HALF, WIDTH, BF16)] * 2, where, grid, w_grid, scalars=1
    )
    got = swap(give)
    mine = jnp.concatenate([keep, got], axis=0)
    mesh_then = after(mesh_latent, mine)
    mesh_first, mesh_third = pair_z(mesh_then, 1), pair_z(mesh_then, 3)

    def far_gather(value):
        return shift(value, False, -1), shift(value, False, 1)

    def give_rows(both, up, down):
        return jnp.concatenate([both[GATHERED:], up[GATHERED:], down[GATHERED:]], axis=0)

    near = [shift(mine, True, step) for step in (-1, 2, 1)]
    ring_0, ring_1 = call(
        ring_kernel, "ring", [shape(2 * GATHERED, COLS, BF16)] * CHUNKS, keep, got, *after(near, (mesh_first, mesh_third))
    )

    mesh_far = pair_z(after(mesh_third, ring_0), 1)
    (down_0, up_0), mesh_far = lax.optimization_barrier((far_gather(ring_0), mesh_far))
    mesh_rows = jnp.concatenate([mesh_latent, mesh_first, mesh_far, mesh_third], axis=0)
    give = [give_rows(ring_0, up_0, down_0)] + [mesh_rows[:, c * COLS : (c + 1) * COLS] for c in both_chunks]
    got_0 = swap(jnp.concatenate(give, axis=0))
    across_0 = shift(up_0[:GATHERED], False, 1), shift(down_0[GATHERED:], False, -1)
    far_1 = far_gather(after(ring_1, up_0))
    edge_terms = call(
        edge_kernel,
        "edge_terms",
        [shape(edges, COLS, F32)] * CHUNKS,
        where,
        live_groups,
        edge_mesh_block,
        pick_recv,
        edge_latent,
        w_mesh,
        w_edge,
        bias.reshape(1, WIDTH),
        mesh_rows,
        got_0,
        scalars=3,
        scratch=[pltpu.VMEM((GROUP, BLOCK, WIDTH), BF16), pltpu.VMEM((GROUP * BLOCK, WIDTH), BF16)],
    )
    cot = dot_t(cotangent, w_node)

    own_across, other_across = lax.optimization_barrier(across_0)
    far_got_0 = swap(other_across)
    (down_1, up_1), edge_terms, got_0, far_got_0 = lax.optimization_barrier((far_1, edge_terms, got_0, far_got_0))
    across_1 = shift(up_1[:GATHERED], False, 1), shift(down_1[GATHERED:], False, -1)

    def forward(chunk, own, got):
        return call(
            forward_kernel,
            f"forward_{chunk}",
            [shape(edges, COLS, F32), shape(RING * HALF, COLS, F32), shape(RING * HALF, COLS, BF16)],
            where,
            live_groups,
            edge_grid_block,
            edge_mesh_block,
            pick_send,
            receiver_offset,
            edge_terms[chunk],
            *own,
            *got,
            scalars=4,
            scratch=[
                pltpu.VMEM((2 * RING * HALF, COLS), F32),
                pltpu.VMEM((SLOTS, BLOCK, COLS), BF16),
                pltpu.SemaphoreType.DMA((SLOTS,)),
            ],
            spec=ANY,
        )

    def pair_sum(*terms):
        outs = [shape(HALF, WIDTH, F32)] + [shape(HALF, WIDTH, BF16)] * 3
        return call(pair_sum_kernel, "pair_sum", outs, *terms)

    def band_sum(own, a, b, c):
        return [own, shift_z(a, 1), shift_z(c, -1), shift_z(b, 2)]

    slope_0, near_sum_0, far_sum_0 = forward(0, (ring_0, up_0, own_across, down_0), (got_0, far_got_0))
    got_1 = swap(give_rows(ring_1, up_1, down_1))
    (own_across, other_across), got_1, far_sum_0, cot = lax.optimization_barrier((across_1, got_1, far_sum_0, cot))
    far_got_1, far_sum_0 = swap(other_across), swap(far_sum_0)
    slope_1, near_sum_1, far_sum_1 = forward(
        1, (ring_1, up_1, own_across, down_1), (got_1, after(far_got_1, far_sum_0))
    )
    sums = band_sum(*pair_sum(near_sum_0, near_sum_1, far_sum_0, swap(far_sum_1)))
    slopes = [slope_0, slope_1]

    aggregate, grads = call(
        node_kernel, "node", [shape(HALF, WIDTH, F32), shape(HALF, WIDTH, BF16)], cot, w_out, *sums
    )

    slots = jnp.arange(SLOTS)
    same = edge_grid_block[:, None] == edge_grid_block[None, :]
    first_of = jnp.min(jnp.where(same, slots[None, :], SLOTS), axis=1).astype(jnp.int32)

    partial_shapes = [shape(GATHERED, COLS, BF16)] * (RING * CHUNKS)
    partial_shapes += [shape(CHUNKS * GATHERED, COLS, BF16), shape(3 * CHUNKS * GATHERED, COLS, BF16)]
    zeros = call(zeros_kernel, "zeros", partial_shapes)
    up, down, across = shift_z(grads, -1), shift_z(grads, 1), shift_z(grads, 2)
    down, zeros = after((down, zeros), up)
    band = [grads, up, across, down]
    inputs = [
        where,
        live_groups,
        edge_grid_block,
        edge_mesh_block,
        first_of,
        pick_recv,
        sender_offset,
        *slopes,
        *band,
        *[swap(p) for p in band],
    ]
    partial = pl.pallas_call(
        backward_kernel,
        in_specs=[SMEM] * 5 + [VMEM] * (len(inputs) - 5) + [VMEM] * len(zeros),
        out_specs=[VMEM] * len(zeros),
        out_shape=partial_shapes,
        input_output_aliases={len(inputs) + i: i for i in range(len(zeros))},
        scratch_shapes=[pltpu.VMEM((SLOTS, BLOCK, WIDTH), F32), pltpu.VMEM((GROUP, BLOCK, WIDTH), BF16)],
        compiler_params=params(),
        cost_estimate=LIGHT,
        name="backward",
    )(*inputs, *zeros)
    own_0, own_1, give_across, give_rest = partial[:RING], partial[RING : 2 * RING], partial[-2], partial[-1]

    def far_send(into, name, terms, *refs):
        kernel = functools.partial(merge_kernel, terms)
        up, down = call(kernel, name, [shape(2 * GATHERED, COLS, BF16)] * 2, *refs, *into)
        return (shift(up, False, 1), shift(down, False, -1)), up

    def column_sum(far, name, terms, *refs):
        kernel = functools.partial(column_sum_kernel, terms)
        outs = [shape(HALF, WIDTH, F32)] + [shape(HALF, WIDTH, BF16)] * 3
        return call(kernel, name, outs, *refs, *far)

    def near_send(here, a, b, c):
        return here, shift(a, True, 1), shift(b, True, 2), shift(c, True, -1)

    def row_sum(name, terms):
        return call(row_sum_kernel, name, [shape(HALF, WIDTH, F32)], w_grid, *terms)[0]

    across = swap(give_across)
    rest = swap(after(give_rest, across))
    into_other = shift(across[:GATHERED], False, 1), shift(across[GATHERED:], False, -1)
    into_mine = shift(own_0[2], False, 1), shift(own_1[2], False, -1)
    step = GATHERED
    far_other, merged = far_send(
        into_other, "merge_other", ((0, step), (0, 4 * step), (0, 2 * step), (0, 5 * step)), rest
    )
    far_mine, merged = far_send(
        after(into_mine, merged), "merge_mine", ((0, 0), (1, 0), (2, 0), (3, 0)), own_0[1], own_1[1], own_0[3], own_1[3]
    )
    activation = jax.nn.silu(aggregate).astype(BF16)
    mesh_out = (mesh_latent.astype(F32) + dot(activation, w_node)).astype(BF16)
    columns = column_sum(after(far_other, (mesh_out, merged)), "column_sum_other", ((0, 0), (0, 3 * step)), rest)
    near_other = near_send(*columns)
    columns = column_sum(after(far_mine, columns), "column_sum_mine", ((0, 0), (1, 0)), own_0[0], own_1[0])
    near_mine = near_send(*columns)
    other = swap(row_sum("row_sum_other", after(near_other, columns)))
    placed = pl.pallas_call(
        place_other_kernel,
        in_specs=[SMEM, VMEM],
        out_specs=ANY,
        out_shape=shape(2 * HALF, WIDTH, F32),
        scratch_shapes=[pltpu.SemaphoreType.DMA],
        compiler_params=params(),
        cost_estimate=LIGHT,
        name="place_other",
    )(where, other)
    grid_grad = pl.pallas_call(
        place_mine_kernel,
        in_specs=[SMEM] + [VMEM] * 5 + [ANY],
        out_specs=ANY,
        out_shape=shape(2 * HALF, WIDTH, F32),
        input_output_aliases={6: 0},
        scratch_shapes=[pltpu.VMEM((HALF, WIDTH), F32), pltpu.SemaphoreType.DMA],
        compiler_params=params(),
        cost_estimate=LIGHT,
        name="place_mine",
    )(where, w_grid, *after(near_mine, placed), placed)
    return (mesh_out, grid_grad)


def solution(mesh):
    split = Mesh(mesh.devices.reshape(4, 2, 4, 4), ("z", "core", "x", "y"))
    rows = P(("z", "core", "x", "y"))
    placed = (rows,) * 8 + (P(),) * 6 + (rows,)
    return jax.shard_map(per_device, mesh=split, in_specs=placed, out_specs=(rows, rows), check_vma=False)
```

```python
import functools

import jax
import jax.numpy as jnp
from jax import lax
from jax.experimental import pallas as pl
from jax.experimental.pallas import tpu as pltpu
from jax.sharding import Mesh
from jax.sharding import PartitionSpec as P

F32 = jnp.float32
BF16 = jnp.bfloat16
RING = 4
BLOCK = 128
SLOTS = 16
GROUP = 4
WIDTH = 512
CHUNKS = 2
COLS = WIDTH // CHUNKS
HALF = 256
GATHERED = RING * HALF
VMEM = pl.BlockSpec(memory_space=pltpu.VMEM)
SMEM = pl.BlockSpec(memory_space=pltpu.SMEM)
ANY = pl.BlockSpec(memory_space=pl.ANY)
LIGHT = pl.CostEstimate(flops=0, bytes_accessed=0, transcendentals=0)
LIMIT = 20 * 1024 * 1024


def shape(rows, cols, dtype):
    return jax.ShapeDtypeStruct((rows, cols), dtype)


def params():
    return pltpu.CompilerParams(vmem_limit_bytes=LIMIT)


CHIP_AXES = ("core", "x", "y")


def along(first, step):
    pairs = []
    for core in range(2):
        for x in range(RING):
            for y in range(RING):
                if (core == 0) == first:
                    to = ((x + step) % RING, y)
                else:
                    to = (x, (y + step) % RING)
                pairs.append((core * 16 + x * RING + y, core * 16 + to[0] * RING + to[1]))
    return pairs


def shift(value, first, step):
    return lax.ppermute(value, CHIP_AXES, along(first, step))


def shift_z(value, step):
    return lax.ppermute(value, "z", [(i, (i + step) % RING) for i in range(RING)])


def after(value, *others):
    return lax.optimization_barrier((value, others))[0]


def pair_z(value, flip):
    return lax.ppermute(value, "z", [(i, i ^ flip) for i in range(RING)])


def swap(value):
    return lax.ppermute(value, "core", [(0, 1), (1, 0)])


def dot(a, b):
    return jnp.dot(a, b, preferred_element_type=F32)


def dot_t(a, b):
    return lax.dot_general(a, b, (((1,), (1,)), ((), ())), preferred_element_type=F32)


def split_dot(a, b, product):
    high = a.astype(BF16)
    low = (a - high.astype(F32)).astype(BF16)
    return product(high, b) + product(low, b)


def sigmoid(value):
    return 0.5 * jnp.tanh(0.5 * value) + 0.5


def one_hot(offsets, slot):
    rows = lax.broadcasted_iota(jnp.int32, (BLOCK, BLOCK), 0)
    return (rows == offsets[pl.ds(slot, 1), :]).astype(BF16)


def grid_place(block, where):
    core, x, y = where[1], where[2], where[3]
    owner = block // 4
    kind = (block % 4) // 2
    dx = lax.rem(x - owner // 4 + RING, RING)
    dy = lax.rem(y - owner % 4 + RING, RING)
    mine = kind == core
    near = jnp.where(kind == 0, dx, dy)
    far = jnp.where(kind == 0, dy, dx)
    return mine, near, far, (block % 2) * BLOCK


def mesh_place(block, where):
    owner = block // 2
    dz = lax.rem(owner // 2 - where[0] + RING, RING)
    return owner % 2 == where[1], dz, (block % 2) * BLOCK


def first_product_kernel(where, grid, w_grid, keep, give):
    core = where[1]
    for out, half in ((give, 1 - core), (keep, core)):
        out[...] = dot(grid[pl.ds(pl.multiple_of(half * HALF, HALF), HALF), :], w_grid[...]).astype(BF16)


def ring_kernel(keep, got, down, across, up, *outs):
    for chunk, out in enumerate(outs):
        cols = pl.ds(chunk * COLS, COLS)
        out[:HALF, :] = keep[:, cols]
        out[GATHERED : GATHERED + HALF, :] = got[:, cols]
        for step, term in enumerate((up, across, down)):
            out[pl.ds((step + 1) * HALF, HALF), :] = term[:HALF, cols]
            out[pl.ds(GATHERED + (step + 1) * HALF, HALF), :] = term[HALF:, cols]


def edge_kernel(where, live, mesh_block, pick, edge, w_mesh, w_edge, bias, *rest):
    pieces, outs, (blocks, rows) = rest[:2], rest[2 : 2 + CHUNKS], rest[-2:]

    @pl.loop(0, live[0])
    def _(group):
        for i in range(GROUP):
            block = mesh_block[group * GROUP + i]
            owner = block // 2
            flip = (owner // 2) ^ where[0]
            mine = owner % 2 == where[1]
            row = flip * HALF + (block % 2) * BLOCK

            @pl.when(mine)
            def _():
                blocks[i] = pieces[0][pl.ds(pl.multiple_of(row, BLOCK), BLOCK), :]

            @pl.when(jnp.logical_not(mine))
            def _():
                for chunk in range(CHUNKS):
                    lines = pl.ds(pl.multiple_of((3 + chunk) * GATHERED + row, BLOCK), BLOCK)
                    blocks[i, :, pl.ds(chunk * COLS, COLS)] = pieces[1][lines, :]

        first = group * GROUP * BLOCK
        for i in range(GROUP):
            at = pl.ds(pl.multiple_of(first + i * BLOCK, BLOCK), BLOCK)
            rows[pl.ds(i * BLOCK, BLOCK), :] = dot(pick[at, :], blocks[i]).astype(BF16)
        lines = pl.ds(pl.multiple_of(first, GROUP * BLOCK), GROUP * BLOCK)
        for chunk in range(CHUNKS):
            cols = pl.ds(chunk * COLS, COLS)
            outs[chunk][lines, :] = dot(rows[...], w_mesh[:, cols]) + dot(edge[lines, :], w_edge[:, cols]) + bias[:, cols]


def forward_kernel(where, live, grid_block, mesh_block, pick, recv, rest_in, *rest):
    pieces, (slope, near, far) = rest[:6], rest[6:9]
    total, blocks, sems = rest[9:]

    @pl.loop(0, live[0] * GROUP)
    def _(slot):
        mine, first, second, row = grid_place(grid_block[slot], where)
        start = first * HALF + row

        def fetch(piece, base):
            lines = pl.ds(pl.multiple_of(base + start, BLOCK), BLOCK)
            pltpu.make_async_copy(pieces[piece].at[lines, :], blocks.at[slot], sems.at[slot]).start()

        for piece in range(RING):

            @pl.when(jnp.logical_and(mine, second == piece))
            def _():
                fetch(piece, 0)

        @pl.when(jnp.logical_and(jnp.logical_not(mine), second != 2))
        def _():
            fetch(RING, jnp.minimum(second, 2) * GATHERED)

        @pl.when(jnp.logical_and(jnp.logical_not(mine), second == 2))
        def _():
            fetch(RING + 1, 0)

    total[...] = jnp.zeros_like(total)

    @pl.loop(0, live[0])
    def _(group):
        slots = [group * GROUP + i for i in range(GROUP)]
        for slot in slots:
            pltpu.make_async_copy(pieces[0].at[pl.ds(0, BLOCK), :], blocks.at[slot], sems.at[slot]).wait()
        for slot in slots:
            at = pl.ds(pl.multiple_of(slot * BLOCK, BLOCK), BLOCK)
            pre = rest_in[at, :] + dot(pick[at, :], blocks[slot])
            sig = sigmoid(pre)
            slope[at, :] = sig * (1.0 + pre * (1.0 - sig))
            value = dot(one_hot(recv, slot), (pre * sig).astype(BF16))
            mine, dz, row = mesh_place(mesh_block[slot], where)
            start = jnp.where(mine, 0, RING * HALF) + dz * HALF + row
            total[pl.ds(pl.multiple_of(start, BLOCK), BLOCK), :] += value

    near[...] = total[: RING * HALF, :]
    far[...] = total[RING * HALF :, :].astype(BF16)


def pair_sum_kernel(*refs):
    near, other, outs = refs[:CHUNKS], refs[CHUNKS : 2 * CHUNKS], refs[2 * CHUNKS :]
    for chunk in range(CHUNKS):
        for step in range(RING):
            lines = pl.ds(step * HALF, HALF)
            value = near[chunk][lines, :] + other[chunk][lines, :].astype(F32)
            outs[step][:, pl.ds(chunk * COLS, COLS)] = value.astype(outs[step].dtype)


def node_kernel(cot, w_out, own, a, b, c, aggregate, grads):
    part = own[...] + (a[...].astype(F32) + b[...].astype(F32) + c[...].astype(F32))
    total = split_dot(part, w_out[...], dot)
    aggregate[...] = total
    sig = sigmoid(total)
    grad = (cot[...] * (sig * (1.0 + total * (1.0 - sig)))).astype(BF16)
    grads[...] = dot_t(grad, w_out[...]).astype(BF16)


def zeros_kernel(*outs):
    for out in outs:
        out[...] = jnp.zeros_like(out)


def backward_kernel(where, live, grid_block, mesh_block, first_of, pick, send, *rest):
    slopes, pieces = rest[:CHUNKS], rest[CHUNKS : CHUNKS + 8]
    outs, (total, blocks) = rest[-2 - RING * CHUNKS - 2 : -2], rest[-2:]

    @pl.loop(0, live[0])
    def _(group):
        slots = [group * GROUP + i for i in range(GROUP)]
        for i, slot in enumerate(slots):
            mine, dz, row = mesh_place(mesh_block[slot], where)
            at = jnp.where(mine, dz, dz + RING)
            for piece in range(8):

                @pl.when(at == piece)
                def _():
                    blocks[i] = pieces[piece][pl.ds(pl.multiple_of(row, BLOCK), BLOCK), :]

        for i, slot in enumerate(slots):
            at = pl.ds(pl.multiple_of(slot * BLOCK, BLOCK), BLOCK)
            hot = one_hot(send, slot)
            first = first_of[slot]
            for c in range(CHUNKS):
                cols = pl.ds(c * COLS, COLS)
                grad = dot(pick[at, :], blocks[i, :, cols]) * slopes[c][at, :]
                part = dot(hot, grad.astype(BF16))
                total[first, :, cols] = jnp.where(first == slot, 0.0, total[first, :, cols]) + part

    @pl.loop(0, live[0] * GROUP)
    def _(slot):
        mine, near, far, row = grid_place(grid_block[slot], where)
        start = lax.rem(RING - near, RING) * HALF + row
        far = lax.rem(RING - far, RING)
        at = jnp.where(first_of[slot] == slot, jnp.where(mine, far, jnp.where(far == 0, RING, RING + 1)), -1)
        for step in range(RING + 2):

            @pl.when(at == step)
            def _():
                for c in range(CHUNKS):
                    if step < RING:
                        to, place = outs[RING * c + step], start
                    elif step == RING:
                        to, place = outs[-2], start + c * GATHERED
                    else:
                        to, place = outs[-1], start + (3 * c + far - 1) * GATHERED
                    to[pl.ds(pl.multiple_of(place, BLOCK), BLOCK), :] = total[slot, :, pl.ds(c * COLS, COLS)].astype(BF16)


def add(a, b):
    return (a[...].astype(F32) + b[...].astype(F32)).astype(BF16)


def merge_kernel(terms, *refs):
    into_down, into_up, out_up, out_down = refs[-4:]
    up_0, up_1, down_0, down_1 = [refs[i].at[pl.ds(base, GATHERED), :] for i, base in terms]
    out_up[:GATHERED, :] = add(up_0, into_up)
    out_up[GATHERED:, :] = up_1[...]
    out_down[:GATHERED, :] = down_0[...]
    out_down[GATHERED:, :] = add(down_1, into_down)


def column_sum_kernel(terms, *refs):
    up, down, here, *outs = refs[-6:]
    for chunk, (i, base) in enumerate(terms):
        cols = pl.ds(chunk * COLS, COLS)
        for step in range(RING):
            both = pl.ds(chunk * GATHERED + step * HALF, HALF)
            value = refs[i][pl.ds(base + step * HALF, HALF), :].astype(F32) + (up[both, :].astype(F32) + down[both, :].astype(F32))
            if step == 0:
                here[:, cols] = value
            else:
                outs[step - 1][:, cols] = value.astype(BF16)


def row_sum_kernel(w_grid, here, up, down, across, out):
    value = here[...] + (up[...].astype(F32) + down[...].astype(F32) + across[...].astype(F32))
    out[...] = split_dot(value, w_grid[...], dot_t)


def place(row, value, out, sem):
    copy = pltpu.make_async_copy(value, out.at[pl.ds(pl.multiple_of(row, HALF), HALF), :], sem)
    copy.start()
    copy.wait()


def place_other_kernel(where, value, placed, out, sem):
    place((1 - where[1]) * HALF, value, out, sem)


def place_mine_kernel(where, w_grid, here, up, down, across, out, value, sem):
    row_sum_kernel(w_grid, here, up, down, across, value)
    place(where[1] * HALF, value, out, sem)


def per_device(
    grid,
    mesh_latent,
    edge_latent,
    edge_grid_block,
    edge_mesh_block,
    sender_offset,
    receiver_offset,
    live_groups,
    w_grid,
    w_mesh,
    w_edge,
    bias,
    w_out,
    w_node,
    cotangent,
):
    def picks(offsets):
        return (offsets.reshape(-1, 1) == jnp.arange(BLOCK, dtype=jnp.int32)).astype(BF16)

    pick_send, pick_recv = picks(sender_offset), picks(receiver_offset)
    where = jnp.stack([lax.axis_index(a) for a in ("z", "core", "x", "y")]).astype(jnp.int32)
    edges = SLOTS * BLOCK
    both_chunks = range(CHUNKS)

    def call(kernel, name, outs, *args, scalars=0, scratch=(), spec=VMEM):
        whole = [SMEM] * scalars + [VMEM] * (len(args) - scalars)
        if spec is ANY:
            whole[-6:] = [ANY] * 6
        return pl.pallas_call(
            kernel,
            in_specs=whole,
            out_specs=[VMEM] * len(outs),
            out_shape=outs,
            scratch_shapes=scratch,
            compiler_params=params(),
            cost_estimate=LIGHT,
            name=name,
        )(*args)

    keep, give = call(
        first_product_kernel, "first_product", [shape(HALF, WIDTH, BF16)] * 2, where, grid, w_grid, scalars=1
    )
    got = swap(give)
    mine = jnp.concatenate([keep, got], axis=0)
    mesh_then = after(mesh_latent, mine)
    mesh_first, mesh_third = pair_z(mesh_then, 1), pair_z(mesh_then, 3)

    def far_gather(value):
        return shift(value, False, -1), shift(value, False, 1)

    def give_rows(both, up, down):
        return jnp.concatenate([both[GATHERED:], up[GATHERED:], down[GATHERED:]], axis=0)

    near = [shift(mine, True, step) for step in (-1, 2, 1)]
    ring_0, ring_1 = call(
        ring_kernel, "ring", [shape(2 * GATHERED, COLS, BF16)] * CHUNKS, keep, got, *after(near, (mesh_first, mesh_third))
    )

    mesh_far = pair_z(after(mesh_third, ring_0), 1)
    (down_0, up_0), mesh_far = lax.optimization_barrier((far_gather(ring_0), mesh_far))
    mesh_rows = jnp.concatenate([mesh_latent, mesh_first, mesh_far, mesh_third], axis=0)
    give = [give_rows(ring_0, up_0, down_0)] + [mesh_rows[:, c * COLS : (c + 1) * COLS] for c in both_chunks]
    got_0 = swap(jnp.concatenate(give, axis=0))
    across_0 = shift(up_0[:GATHERED], False, 1), shift(down_0[GATHERED:], False, -1)
    far_1 = far_gather(after(ring_1, up_0))
    edge_terms = call(
        edge_kernel,
        "edge_terms",
        [shape(edges, COLS, F32)] * CHUNKS,
        where,
        live_groups,
        edge_mesh_block,
        pick_recv,
        edge_latent,
        w_mesh,
        w_edge,
        bias.reshape(1, WIDTH),
        mesh_rows,
        got_0,
        scalars=3,
        scratch=[pltpu.VMEM((GROUP, BLOCK, WIDTH), BF16), pltpu.VMEM((GROUP * BLOCK, WIDTH), BF16)],
    )
    cot = dot_t(cotangent, w_node)

    own_across, other_across = lax.optimization_barrier(across_0)
    far_got_0 = swap(other_across)
    (down_1, up_1), edge_terms, got_0, far_got_0 = lax.optimization_barrier((far_1, edge_terms, got_0, far_got_0))
    across_1 = shift(down_1[GATHERED:], False, -1), shift(up_1[:GATHERED], False, 1)

    def forward(chunk, own, got):
        return call(
            forward_kernel,
            f"forward_{chunk}",
            [shape(edges, COLS, F32), shape(RING * HALF, COLS, F32), shape(RING * HALF, COLS, BF16)],
            where,
            live_groups,
            edge_grid_block,
            edge_mesh_block,
            pick_send,
            receiver_offset,
            edge_terms[chunk],
            *own,
            *got,
            scalars=4,
            scratch=[
                pltpu.VMEM((2 * RING * HALF, COLS), F32),
                pltpu.VMEM((SLOTS, BLOCK, COLS), BF16),
                pltpu.SemaphoreType.DMA((SLOTS,)),
            ],
            spec=ANY,
        )

    def pair_sum(*terms):
        outs = [shape(HALF, WIDTH, F32)] + [shape(HALF, WIDTH, BF16)] * 3
        return call(pair_sum_kernel, "pair_sum", outs, *terms)

    def band_sum(own, a, b, c):
        return [own, shift_z(a, 1), shift_z(c, -1), shift_z(b, 2)]

    slope_0, near_sum_0, far_sum_0 = forward(0, (ring_0, up_0, own_across, down_0), (got_0, far_got_0))
    got_1 = swap(give_rows(ring_1, up_1, down_1))
    (other_across, own_across), got_1, far_sum_0, cot = lax.optimization_barrier((across_1, got_1, far_sum_0, cot))
    far_got_1, far_sum_0 = swap(other_across), swap(far_sum_0)
    slope_1, near_sum_1, far_sum_1 = forward(
        1, (ring_1, up_1, own_across, down_1), (got_1, after(far_got_1, far_sum_0))
    )
    sums = band_sum(*pair_sum(near_sum_0, near_sum_1, far_sum_0, swap(far_sum_1)))
    slopes = [slope_0, slope_1]

    aggregate, grads = call(
        node_kernel, "node", [shape(HALF, WIDTH, F32), shape(HALF, WIDTH, BF16)], cot, w_out, *sums
    )

    slots = jnp.arange(SLOTS)
    same = edge_grid_block[:, None] == edge_grid_block[None, :]
    first_of = jnp.min(jnp.where(same, slots[None, :], SLOTS), axis=1).astype(jnp.int32)

    partial_shapes = [shape(GATHERED, COLS, BF16)] * (RING * CHUNKS)
    partial_shapes += [shape(CHUNKS * GATHERED, COLS, BF16), shape(3 * CHUNKS * GATHERED, COLS, BF16)]
    zeros = call(zeros_kernel, "zeros", partial_shapes)
    up, down, across = shift_z(grads, -1), shift_z(grads, 1), shift_z(grads, 2)
    down, zeros = after((down, zeros), up)
    band = [grads, up, across, down]
    inputs = [
        where,
        live_groups,
        edge_grid_block,
        edge_mesh_block,
        first_of,
        pick_recv,
        sender_offset,
        *slopes,
        *band,
        *[swap(p) for p in band],
    ]
    partial = pl.pallas_call(
        backward_kernel,
        in_specs=[SMEM] * 5 + [VMEM] * (len(inputs) - 5) + [VMEM] * len(zeros),
        out_specs=[VMEM] * len(zeros),
        out_shape=partial_shapes,
        input_output_aliases={len(inputs) + i: i for i in range(len(zeros))},
        scratch_shapes=[pltpu.VMEM((SLOTS, BLOCK, WIDTH), F32), pltpu.VMEM((GROUP, BLOCK, WIDTH), BF16)],
        compiler_params=params(),
        cost_estimate=LIGHT,
        name="backward",
    )(*inputs, *zeros)
    own_0, own_1, give_here, give_far = partial[:RING], partial[RING : 2 * RING], partial[-2], partial[-1]

    def far_send(into, name, terms, *refs):
        kernel = functools.partial(merge_kernel, terms)
        up, down = call(kernel, name, [shape(2 * GATHERED, COLS, BF16)] * 2, *refs, *into)
        return (shift(down, False, -1), shift(up, False, 1)), up

    def column_sum(far, name, terms, *refs):
        kernel = functools.partial(column_sum_kernel, terms)
        outs = [shape(HALF, WIDTH, F32)] + [shape(HALF, WIDTH, BF16)] * 3
        return call(kernel, name, outs, *refs, *far)

    def near_send(here, a, b, c):
        return here, shift(a, True, 1), shift(b, True, 2), shift(c, True, -1)

    def row_sum(name, terms):
        return call(row_sum_kernel, name, [shape(HALF, WIDTH, F32)], w_grid, *terms)[0]

    step = GATHERED
    into_mine = shift(own_1[2], False, -1), shift(own_0[2], False, 1)
    given = swap(give_far)
    into_other = [shift(given[step : 2 * step], False, 1), shift(given[4 * step : 5 * step], False, -1)]
    far_mine, merged = far_send(
        into_mine, "merge_mine", ((0, 0), (1, 0), (2, 0), (3, 0)), own_0[1], own_1[1], own_0[3], own_1[3]
    )
    far_other, merged = far_send(
        after(into_other, merged)[::-1], "merge_other", ((0, 0), (0, 3 * step), (0, 2 * step), (0, 5 * step)), given
    )
    given_here = swap(after(give_here, merged))
    activation = jax.nn.silu(aggregate).astype(BF16)
    mesh_out = (mesh_latent.astype(F32) + dot(activation, w_node)).astype(BF16)
    columns = column_sum(after(far_mine, (mesh_out, merged, given_here)), "column_sum_mine", ((0, 0), (1, 0)), own_0[0], own_1[0])
    near_mine = near_send(*columns)
    columns = column_sum(after(far_other, columns), "column_sum_other", ((0, 0), (0, step)), given_here)
    near_other = near_send(*columns)
    placed = pl.pallas_call(
        place_mine_kernel,
        in_specs=[SMEM] + [VMEM] * 5,
        out_specs=ANY,
        out_shape=shape(2 * HALF, WIDTH, F32),
        scratch_shapes=[pltpu.VMEM((HALF, WIDTH), F32), pltpu.SemaphoreType.DMA],
        compiler_params=params(),
        cost_estimate=LIGHT,
        name="place_mine",
    )(where, w_grid, *after(near_mine, columns))
    other = swap(row_sum("row_sum_other", after(near_other, placed)))
    grid_grad = pl.pallas_call(
        place_other_kernel,
        in_specs=[SMEM, VMEM, ANY],
        out_specs=ANY,
        out_shape=shape(2 * HALF, WIDTH, F32),
        input_output_aliases={2: 0},
        scratch_shapes=[pltpu.SemaphoreType.DMA],
        compiler_params=params(),
        cost_estimate=LIGHT,
        name="place_other",
    )(where, other, placed)
    return (mesh_out, grid_grad)


def solution(mesh):
    split = Mesh(mesh.devices.reshape(4, 2, 4, 4), ("z", "core", "x", "y"))
    rows = P(("z", "core", "x", "y"))
    placed = (rows,) * 8 + (P(),) * 6 + (rows,)
    return jax.shard_map(per_device, mesh=split, in_specs=placed, out_specs=(rows, rows), check_vma=False)
```

```python
import functools

import jax
import jax.numpy as jnp
from jax import lax
from jax.experimental import pallas as pl
from jax.experimental.pallas import tpu as pltpu
from jax.sharding import Mesh
from jax.sharding import PartitionSpec as P

F32 = jnp.float32
BF16 = jnp.bfloat16
RING = 4
BLOCK = 128
SLOTS = 16
GROUP = 4
WIDTH = 512
CHUNKS = 2
COLS = WIDTH // CHUNKS
HALF = 256
GATHERED = RING * HALF
VMEM = pl.BlockSpec(memory_space=pltpu.VMEM)
SMEM = pl.BlockSpec(memory_space=pltpu.SMEM)
ANY = pl.BlockSpec(memory_space=pl.ANY)
LIGHT = pl.CostEstimate(flops=0, bytes_accessed=0, transcendentals=0)
LIMIT = 20 * 1024 * 1024


def shape(rows, cols, dtype):
    return jax.ShapeDtypeStruct((rows, cols), dtype)


def params():
    return pltpu.CompilerParams(vmem_limit_bytes=LIMIT)


CHIP_AXES = ("core", "x", "y")


def along(first, step):
    pairs = []
    for core in range(2):
        for x in range(RING):
            for y in range(RING):
                if (core == 0) == first:
                    to = ((x + step) % RING, y)
                else:
                    to = (x, (y + step) % RING)
                pairs.append((core * 16 + x * RING + y, core * 16 + to[0] * RING + to[1]))
    return pairs


def shift(value, first, step):
    return lax.ppermute(value, CHIP_AXES, along(first, step))


def shift_z(value, step):
    return lax.ppermute(value, "z", [(i, (i + step) % RING) for i in range(RING)])


def after(value, *others):
    return lax.optimization_barrier((value, others))[0]


def pair_z(value, flip):
    return lax.ppermute(value, "z", [(i, i ^ flip) for i in range(RING)])


def swap(value):
    return lax.ppermute(value, "core", [(0, 1), (1, 0)])


def dot(a, b):
    return jnp.dot(a, b, preferred_element_type=F32)


def dot_t(a, b):
    return lax.dot_general(a, b, (((1,), (1,)), ((), ())), preferred_element_type=F32)


def split_dot(a, b, product):
    high = a.astype(BF16)
    low = (a - high.astype(F32)).astype(BF16)
    return product(high, b) + product(low, b)


def sigmoid(value):
    return 0.5 * jnp.tanh(0.5 * value) + 0.5


def one_hot(offsets, slot):
    rows = lax.broadcasted_iota(jnp.int32, (BLOCK, BLOCK), 0)
    return (rows == offsets[pl.ds(slot, 1), :]).astype(BF16)


def grid_place(block, where):
    core, x, y = where[1], where[2], where[3]
    owner = block // 4
    kind = (block % 4) // 2
    dx = lax.rem(x - owner // 4 + RING, RING)
    dy = lax.rem(y - owner % 4 + RING, RING)
    mine = kind == core
    near = jnp.where(kind == 0, dx, dy)
    far = jnp.where(kind == 0, dy, dx)
    return mine, near, far, (block % 2) * BLOCK


def mesh_place(block, where):
    owner = block // 2
    dz = lax.rem(owner // 2 - where[0] + RING, RING)
    return owner % 2 == where[1], dz, (block % 2) * BLOCK


def first_product_kernel(where, grid, w_grid, keep, give):
    core = where[1]
    for out, half in ((give, 1 - core), (keep, core)):
        out[...] = dot(grid[pl.ds(pl.multiple_of(half * HALF, HALF), HALF), :], w_grid[...]).astype(BF16)


def ring_kernel(keep, got, down, across, up, *outs):
    for chunk, out in enumerate(outs):
        cols = pl.ds(chunk * COLS, COLS)
        out[:HALF, :] = keep[:, cols]
        out[GATHERED : GATHERED + HALF, :] = got[:, cols]
        for step, term in enumerate((up, across, down)):
            out[pl.ds((step + 1) * HALF, HALF), :] = term[:HALF, cols]
            out[pl.ds(GATHERED + (step + 1) * HALF, HALF), :] = term[HALF:, cols]


def edge_kernel(where, live, mesh_block, pick, edge, w_mesh, w_edge, bias, *rest):
    pieces, outs, (blocks, rows) = rest[:2], rest[2 : 2 + CHUNKS], rest[-2:]

    @pl.loop(0, live[0])
    def _(group):
        for i in range(GROUP):
            block = mesh_block[group * GROUP + i]
            owner = block // 2
            flip = (owner // 2) ^ where[0]
            mine = owner % 2 == where[1]
            row = flip * HALF + (block % 2) * BLOCK

            @pl.when(mine)
            def _():
                blocks[i] = pieces[0][pl.ds(pl.multiple_of(row, BLOCK), BLOCK), :]

            @pl.when(jnp.logical_not(mine))
            def _():
                for chunk in range(CHUNKS):
                    lines = pl.ds(pl.multiple_of((3 + chunk) * GATHERED + row, BLOCK), BLOCK)
                    blocks[i, :, pl.ds(chunk * COLS, COLS)] = pieces[1][lines, :]

        first = group * GROUP * BLOCK
        for i in range(GROUP):
            at = pl.ds(pl.multiple_of(first + i * BLOCK, BLOCK), BLOCK)
            rows[pl.ds(i * BLOCK, BLOCK), :] = dot(pick[at, :], blocks[i]).astype(BF16)
        lines = pl.ds(pl.multiple_of(first, GROUP * BLOCK), GROUP * BLOCK)
        for chunk in range(CHUNKS):
            cols = pl.ds(chunk * COLS, COLS)
            outs[chunk][lines, :] = dot(rows[...], w_mesh[:, cols]) + dot(edge[lines, :], w_edge[:, cols]) + bias[:, cols]


def forward_kernel(where, live, grid_block, mesh_block, pick, recv, rest_in, *rest):
    pieces, (slope, near, far) = rest[:6], rest[6:9]
    total, blocks, sems = rest[9:]

    @pl.loop(0, live[0] * GROUP)
    def _(slot):
        mine, first, second, row = grid_place(grid_block[slot], where)
        start = first * HALF + row

        def fetch(piece, base):
            lines = pl.ds(pl.multiple_of(base + start, BLOCK), BLOCK)
            pltpu.make_async_copy(pieces[piece].at[lines, :], blocks.at[slot], sems.at[slot]).start()

        for piece in range(RING):

            @pl.when(jnp.logical_and(mine, second == piece))
            def _():
                fetch(piece, 0)

        @pl.when(jnp.logical_and(jnp.logical_not(mine), second != 2))
        def _():
            fetch(RING, jnp.minimum(second, 2) * GATHERED)

        @pl.when(jnp.logical_and(jnp.logical_not(mine), second == 2))
        def _():
            fetch(RING + 1, 0)

    total[...] = jnp.zeros_like(total)

    @pl.loop(0, live[0])
    def _(group):
        slots = [group * GROUP + i for i in range(GROUP)]
        for slot in slots:
            pltpu.make_async_copy(pieces[0].at[pl.ds(0, BLOCK), :], blocks.at[slot], sems.at[slot]).wait()
        for slot in slots:
            at = pl.ds(pl.multiple_of(slot * BLOCK, BLOCK), BLOCK)
            pre = rest_in[at, :] + dot(pick[at, :], blocks[slot])
            sig = sigmoid(pre)
            slope[at, :] = sig * (1.0 + pre * (1.0 - sig))
            value = dot(one_hot(recv, slot), (pre * sig).astype(BF16))
            mine, dz, row = mesh_place(mesh_block[slot], where)
            start = jnp.where(mine, 0, RING * HALF) + dz * HALF + row
            total[pl.ds(pl.multiple_of(start, BLOCK), BLOCK), :] += value

    near[...] = total[: RING * HALF, :]
    far[...] = total[RING * HALF :, :].astype(BF16)


def pair_sum_kernel(*refs):
    near, other, outs = refs[:CHUNKS], refs[CHUNKS : 2 * CHUNKS], refs[2 * CHUNKS :]
    for chunk in range(CHUNKS):
        for step in range(RING):
            lines = pl.ds(step * HALF, HALF)
            value = near[chunk][lines, :] + other[chunk][lines, :].astype(F32)
            outs[step][:, pl.ds(chunk * COLS, COLS)] = value.astype(outs[step].dtype)


def node_kernel(cot, w_out, own, a, b, c, aggregate, grads):
    part = own[...] + (a[...].astype(F32) + b[...].astype(F32) + c[...].astype(F32))
    total = split_dot(part, w_out[...], dot)
    aggregate[...] = total
    sig = sigmoid(total)
    grad = (cot[...] * (sig * (1.0 + total * (1.0 - sig)))).astype(BF16)
    grads[...] = dot_t(grad, w_out[...]).astype(BF16)


def zeros_kernel(*outs):
    for out in outs:
        out[...] = jnp.zeros_like(out)


def backward_kernel(where, live, grid_block, mesh_block, first_of, pick, send, *rest):
    slopes, pieces = rest[:CHUNKS], rest[CHUNKS : CHUNKS + 8]
    outs, (total, blocks) = rest[-2 - RING * CHUNKS - 2 : -2], rest[-2:]

    @pl.loop(0, live[0])
    def _(group):
        slots = [group * GROUP + i for i in range(GROUP)]
        for i, slot in enumerate(slots):
            mine, dz, row = mesh_place(mesh_block[slot], where)
            at = jnp.where(mine, dz, dz + RING)
            for piece in range(8):

                @pl.when(at == piece)
                def _():
                    blocks[i] = pieces[piece][pl.ds(pl.multiple_of(row, BLOCK), BLOCK), :]

        for i, slot in enumerate(slots):
            at = pl.ds(pl.multiple_of(slot * BLOCK, BLOCK), BLOCK)
            hot = one_hot(send, slot)
            first = first_of[slot]
            for c in range(CHUNKS):
                cols = pl.ds(c * COLS, COLS)
                grad = dot(pick[at, :], blocks[i, :, cols]) * slopes[c][at, :]
                part = dot(hot, grad.astype(BF16))
                total[first, :, cols] = jnp.where(first == slot, 0.0, total[first, :, cols]) + part

    @pl.loop(0, live[0] * GROUP)
    def _(slot):
        mine, near, far, row = grid_place(grid_block[slot], where)
        start = lax.rem(RING - near, RING) * HALF + row
        far = lax.rem(RING - far, RING)
        at = jnp.where(first_of[slot] == slot, jnp.where(mine, far, jnp.where(far == 0, RING, RING + 1)), -1)
        for step in range(RING + 2):

            @pl.when(at == step)
            def _():
                for c in range(CHUNKS):
                    if step < RING:
                        to, place = outs[RING * c + step], start
                    elif step == RING:
                        to, place = outs[-2], start + c * GATHERED
                    else:
                        to, place = outs[-1], start + (3 * c + far - 1) * GATHERED
                    to[pl.ds(pl.multiple_of(place, BLOCK), BLOCK), :] = total[slot, :, pl.ds(c * COLS, COLS)].astype(BF16)


def add(a, b):
    return (a[...].astype(F32) + b[...].astype(F32)).astype(BF16)


def merge_kernel(terms, *refs):
    into_down, into_up, out_up, out_down = refs[-4:]
    up_0, up_1, down_0, down_1 = [refs[i].at[pl.ds(base, GATHERED), :] for i, base in terms]
    out_up[:GATHERED, :] = add(up_0, into_up)
    out_up[GATHERED:, :] = up_1[...]
    out_down[:GATHERED, :] = down_0[...]
    out_down[GATHERED:, :] = add(down_1, into_down)


def column_sum_kernel(terms, *refs):
    up, down, here, *outs = refs[-6:]
    for chunk, (i, base) in enumerate(terms):
        cols = pl.ds(chunk * COLS, COLS)
        for step in range(RING):
            both = pl.ds(chunk * GATHERED + step * HALF, HALF)
            value = refs[i][pl.ds(base + step * HALF, HALF), :].astype(F32) + (up[both, :].astype(F32) + down[both, :].astype(F32))
            if step == 0:
                here[:, cols] = value
            else:
                outs[step - 1][:, cols] = value.astype(BF16)


def row_sum_kernel(w_grid, here, up, down, across, out):
    value = here[...] + (up[...].astype(F32) + down[...].astype(F32) + across[...].astype(F32))
    out[...] = split_dot(value, w_grid[...], dot_t)


def place(row, value, out, sem):
    copy = pltpu.make_async_copy(value, out.at[pl.ds(pl.multiple_of(row, HALF), HALF), :], sem)
    copy.start()
    copy.wait()


def place_other_kernel(where, value, placed, out, sem):
    place((1 - where[1]) * HALF, value, out, sem)


def place_mine_kernel(where, w_grid, here, up, down, across, out, value, sem):
    row_sum_kernel(w_grid, here, up, down, across, value)
    place(where[1] * HALF, value, out, sem)


def per_device(
    grid,
    mesh_latent,
    edge_latent,
    edge_grid_block,
    edge_mesh_block,
    sender_offset,
    receiver_offset,
    live_groups,
    w_grid,
    w_mesh,
    w_edge,
    bias,
    w_out,
    w_node,
    cotangent,
):
    def picks(offsets):
        return (offsets.reshape(-1, 1) == jnp.arange(BLOCK, dtype=jnp.int32)).astype(BF16)

    pick_send, pick_recv = picks(sender_offset), picks(receiver_offset)
    where = jnp.stack([lax.axis_index(a) for a in ("z", "core", "x", "y")]).astype(jnp.int32)
    edges = SLOTS * BLOCK
    both_chunks = range(CHUNKS)

    def call(kernel, name, outs, *args, scalars=0, scratch=(), spec=VMEM):
        whole = [SMEM] * scalars + [VMEM] * (len(args) - scalars)
        if spec is ANY:
            whole[-6:] = [ANY] * 6
        return pl.pallas_call(
            kernel,
            in_specs=whole,
            out_specs=[VMEM] * len(outs),
            out_shape=outs,
            scratch_shapes=scratch,
            compiler_params=params(),
            cost_estimate=LIGHT,
            name=name,
        )(*args)

    keep, give = call(
        first_product_kernel, "first_product", [shape(HALF, WIDTH, BF16)] * 2, where, grid, w_grid, scalars=1
    )
    got = swap(give)
    mine = jnp.concatenate([keep, got], axis=0)
    mesh_then = after(mesh_latent, mine)
    mesh_first, mesh_third = pair_z(mesh_then, 1), pair_z(mesh_then, 3)

    def far_gather(value):
        return shift(value, False, -1), shift(value, False, 1)

    def give_rows(both, up, down):
        return jnp.concatenate([both[GATHERED:], up[GATHERED:], down[GATHERED:]], axis=0)

    near = [shift(mine, True, step) for step in (-1, 2, 1)]
    ring_0, ring_1 = call(
        ring_kernel, "ring", [shape(2 * GATHERED, COLS, BF16)] * CHUNKS, keep, got, *after(near, (mesh_first, mesh_third))
    )

    mesh_far = pair_z(after(mesh_third, ring_0), 1)
    (down_0, up_0), mesh_far = lax.optimization_barrier((far_gather(ring_0), mesh_far))
    mesh_rows = jnp.concatenate([mesh_latent, mesh_first, mesh_far, mesh_third], axis=0)
    give = [give_rows(ring_0, up_0, down_0)] + [mesh_rows[:, c * COLS : (c + 1) * COLS] for c in both_chunks]
    got_0 = swap(jnp.concatenate(give, axis=0))
    across_0 = shift(up_0[:GATHERED], False, 1), shift(down_0[GATHERED:], False, -1)
    far_1 = far_gather(after(ring_1, up_0))
    edge_terms = call(
        edge_kernel,
        "edge_terms",
        [shape(edges, COLS, F32)] * CHUNKS,
        where,
        live_groups,
        edge_mesh_block,
        pick_recv,
        edge_latent,
        w_mesh,
        w_edge,
        bias.reshape(1, WIDTH),
        mesh_rows,
        got_0,
        scalars=3,
        scratch=[pltpu.VMEM((GROUP, BLOCK, WIDTH), BF16), pltpu.VMEM((GROUP * BLOCK, WIDTH), BF16)],
    )
    cot = dot_t(cotangent, w_node)

    own_across, other_across = lax.optimization_barrier(across_0)
    far_got_0 = swap(other_across)
    (down_1, up_1), edge_terms, got_0, far_got_0 = lax.optimization_barrier((far_1, edge_terms, got_0, far_got_0))
    across_1 = shift(down_1[GATHERED:], False, -1), shift(up_1[:GATHERED], False, 1)

    def forward(chunk, own, got):
        return call(
            forward_kernel,
            f"forward_{chunk}",
            [shape(edges, COLS, F32), shape(RING * HALF, COLS, F32), shape(RING * HALF, COLS, BF16)],
            where,
            live_groups,
            edge_grid_block,
            edge_mesh_block,
            pick_send,
            receiver_offset,
            edge_terms[chunk],
            *own,
            *got,
            scalars=4,
            scratch=[
                pltpu.VMEM((2 * RING * HALF, COLS), F32),
                pltpu.VMEM((SLOTS, BLOCK, COLS), BF16),
                pltpu.SemaphoreType.DMA((SLOTS,)),
            ],
            spec=ANY,
        )

    def pair_sum(*terms):
        outs = [shape(HALF, WIDTH, F32)] + [shape(HALF, WIDTH, BF16)] * 3
        return call(pair_sum_kernel, "pair_sum", outs, *terms)

    def band_sum(own, a, b, c):
        return [own, shift_z(a, 1), shift_z(c, -1), shift_z(b, 2)]

    slope_0, near_sum_0, far_sum_0 = forward(0, (ring_0, up_0, own_across, down_0), (got_0, far_got_0))
    got_1 = swap(give_rows(ring_1, up_1, down_1))
    (other_across, own_across), got_1, far_sum_0, cot = lax.optimization_barrier((across_1, got_1, far_sum_0, cot))
    far_got_1, far_sum_0 = swap(other_across), swap(far_sum_0)
    slope_1, near_sum_1, far_sum_1 = forward(
        1, (ring_1, up_1, own_across, down_1), (got_1, far_got_1)
    )
    sums = band_sum(*pair_sum(near_sum_0, near_sum_1, far_sum_0, swap(far_sum_1)))
    slopes = [slope_0, slope_1]

    aggregate, grads = call(
        node_kernel, "node", [shape(HALF, WIDTH, F32), shape(HALF, WIDTH, BF16)], cot, w_out, *sums
    )

    slots = jnp.arange(SLOTS)
    same = edge_grid_block[:, None] == edge_grid_block[None, :]
    first_of = jnp.min(jnp.where(same, slots[None, :], SLOTS), axis=1).astype(jnp.int32)

    partial_shapes = [shape(GATHERED, COLS, BF16)] * (RING * CHUNKS)
    partial_shapes += [shape(CHUNKS * GATHERED, COLS, BF16), shape(3 * CHUNKS * GATHERED, COLS, BF16)]
    zeros = call(zeros_kernel, "zeros", partial_shapes)
    up, down, across = shift_z(grads, -1), shift_z(grads, 1), shift_z(grads, 2)
    down, zeros = after((down, zeros), up)
    band = [grads, up, across, down]
    inputs = [
        where,
        live_groups,
        edge_grid_block,
        edge_mesh_block,
        first_of,
        pick_recv,
        sender_offset,
        *slopes,
        *band,
        *[swap(p) for p in band],
    ]
    partial = pl.pallas_call(
        backward_kernel,
        in_specs=[SMEM] * 5 + [VMEM] * (len(inputs) - 5) + [VMEM] * len(zeros),
        out_specs=[VMEM] * len(zeros),
        out_shape=partial_shapes,
        input_output_aliases={len(inputs) + i: i for i in range(len(zeros))},
        scratch_shapes=[pltpu.VMEM((SLOTS, BLOCK, WIDTH), F32), pltpu.VMEM((GROUP, BLOCK, WIDTH), BF16)],
        compiler_params=params(),
        cost_estimate=LIGHT,
        name="backward",
    )(*inputs, *zeros)
    own_0, own_1, give_here, give_far = partial[:RING], partial[RING : 2 * RING], partial[-2], partial[-1]

    def far_send(into, name, terms, *refs):
        kernel = functools.partial(merge_kernel, terms)
        up, down = call(kernel, name, [shape(2 * GATHERED, COLS, BF16)] * 2, *refs, *into)
        return (shift(down, False, -1), shift(up, False, 1)), up

    def column_sum(far, name, terms, *refs):
        kernel = functools.partial(column_sum_kernel, terms)
        outs = [shape(HALF, WIDTH, F32)] + [shape(HALF, WIDTH, BF16)] * 3
        return call(kernel, name, outs, *refs, *far)

    def near_send(here, a, b, c):
        return here, shift(a, True, 1), shift(b, True, 2), shift(c, True, -1)

    def row_sum(name, terms):
        return call(row_sum_kernel, name, [shape(HALF, WIDTH, F32)], w_grid, *terms)[0]

    step = GATHERED
    into_mine = shift(own_1[2], False, -1), shift(own_0[2], False, 1)
    given = swap(give_far)
    into_other = [shift(given[step : 2 * step], False, 1), shift(given[4 * step : 5 * step], False, -1)]
    far_mine, merged = far_send(
        into_mine, "merge_mine", ((0, 0), (1, 0), (2, 0), (3, 0)), own_0[1], own_1[1], own_0[3], own_1[3]
    )
    far_other, merged = far_send(
        after(into_other, merged)[::-1], "merge_other", ((0, 0), (0, 3 * step), (0, 2 * step), (0, 5 * step)), given
    )
    given_here = swap(after(give_here, merged))
    activation = jax.nn.silu(aggregate).astype(BF16)
    mesh_out = (mesh_latent.astype(F32) + dot(activation, w_node)).astype(BF16)
    columns = column_sum(after(far_mine, (mesh_out, merged, given_here)), "column_sum_mine", ((0, 0), (1, 0)), own_0[0], own_1[0])
    near_mine = near_send(*columns)
    columns = column_sum(after(far_other, columns), "column_sum_other", ((0, 0), (0, step)), given_here)
    near_other = near_send(*columns)
    placed = pl.pallas_call(
        place_mine_kernel,
        in_specs=[SMEM] + [VMEM] * 5,
        out_specs=ANY,
        out_shape=shape(2 * HALF, WIDTH, F32),
        scratch_shapes=[pltpu.VMEM((HALF, WIDTH), F32), pltpu.SemaphoreType.DMA],
        compiler_params=params(),
        cost_estimate=LIGHT,
        name="place_mine",
    )(where, w_grid, *after(near_mine, columns))
    other = swap(row_sum("row_sum_other", after(near_other, placed)))
    grid_grad = pl.pallas_call(
        place_other_kernel,
        in_specs=[SMEM, VMEM, ANY],
        out_specs=ANY,
        out_shape=shape(2 * HALF, WIDTH, F32),
        input_output_aliases={2: 0},
        scratch_shapes=[pltpu.SemaphoreType.DMA],
        compiler_params=params(),
        cost_estimate=LIGHT,
        name="place_other",
    )(where, other, placed)
    return (mesh_out, grid_grad)


def solution(mesh):
    split = Mesh(mesh.devices.reshape(4, 2, 4, 4), ("z", "core", "x", "y"))
    rows = P(("z", "core", "x", "y"))
    placed = (rows,) * 8 + (P(),) * 6 + (rows,)
    return jax.shard_map(per_device, mesh=split, in_specs=placed, out_specs=(rows, rows), check_vma=False)
```

```python
import functools

import jax
import jax.numpy as jnp
from jax import lax
from jax.experimental import pallas as pl
from jax.experimental.pallas import tpu as pltpu
from jax.sharding import Mesh
from jax.sharding import PartitionSpec as P

F32 = jnp.float32
BF16 = jnp.bfloat16
RING = 4
BLOCK = 128
SLOTS = 16
GROUP = 4
WIDTH = 512
CHUNKS = 2
COLS = WIDTH // CHUNKS
HALF = 256
GATHERED = RING * HALF
VMEM = pl.BlockSpec(memory_space=pltpu.VMEM)
SMEM = pl.BlockSpec(memory_space=pltpu.SMEM)
ANY = pl.BlockSpec(memory_space=pl.ANY)
LIGHT = pl.CostEstimate(flops=0, bytes_accessed=0, transcendentals=0)
LIMIT = 20 * 1024 * 1024


def shape(rows, cols, dtype):
    return jax.ShapeDtypeStruct((rows, cols), dtype)


def params():
    return pltpu.CompilerParams(vmem_limit_bytes=LIMIT)


CHIP_AXES = ("core", "x", "y")


def along(first, step):
    pairs = []
    for core in range(2):
        for x in range(RING):
            for y in range(RING):
                if (core == 0) == first:
                    to = ((x + step) % RING, y)
                else:
                    to = (x, (y + step) % RING)
                pairs.append((core * 16 + x * RING + y, core * 16 + to[0] * RING + to[1]))
    return pairs


def shift(value, first, step):
    return lax.ppermute(value, CHIP_AXES, along(first, step))


def shift_z(value, step):
    return lax.ppermute(value, "z", [(i, (i + step) % RING) for i in range(RING)])


def after(value, *others):
    return lax.optimization_barrier((value, others))[0]


def pair_z(value, flip):
    return lax.ppermute(value, "z", [(i, i ^ flip) for i in range(RING)])


def swap(value):
    return lax.ppermute(value, "core", [(0, 1), (1, 0)])


def dot(a, b):
    return jnp.dot(a, b, preferred_element_type=F32)


def dot_t(a, b):
    return lax.dot_general(a, b, (((1,), (1,)), ((), ())), preferred_element_type=F32)


def split_dot(a, b, product):
    high = a.astype(BF16)
    low = (a - high.astype(F32)).astype(BF16)
    return product(high, b) + product(low, b)


def sigmoid(value):
    return 0.5 * jnp.tanh(0.5 * value) + 0.5


def one_hot(offsets, slot):
    rows = lax.broadcasted_iota(jnp.int32, (BLOCK, BLOCK), 0)
    return (rows == offsets[pl.ds(slot, 1), :]).astype(BF16)


def grid_place(block, where):
    core, x, y = where[1], where[2], where[3]
    owner = block // 4
    kind = (block % 4) // 2
    dx = lax.rem(x - owner // 4 + RING, RING)
    dy = lax.rem(y - owner % 4 + RING, RING)
    mine = kind == core
    near = jnp.where(kind == 0, dx, dy)
    far = jnp.where(kind == 0, dy, dx)
    return mine, near, far, (block % 2) * BLOCK


def mesh_place(block, where):
    owner = block // 2
    dz = lax.rem(owner // 2 - where[0] + RING, RING)
    return owner % 2 == where[1], dz, (block % 2) * BLOCK


def first_product_kernel(where, grid, w_grid, keep, give):
    core = where[1]
    for out, half in ((give, 1 - core), (keep, core)):
        out[...] = dot(grid[pl.ds(pl.multiple_of(half * HALF, HALF), HALF), :], w_grid[...]).astype(BF16)


def ring_kernel(keep, got, down, across, up, *outs):
    for chunk, out in enumerate(outs):
        cols = pl.ds(chunk * COLS, COLS)
        out[:HALF, :] = keep[:, cols]
        out[GATHERED : GATHERED + HALF, :] = got[:, cols]
        for step, term in enumerate((up, across, down)):
            out[pl.ds((step + 1) * HALF, HALF), :] = term[:HALF, cols]
            out[pl.ds(GATHERED + (step + 1) * HALF, HALF), :] = term[HALF:, cols]


def edge_kernel(where, live, mesh_block, pick, edge, w_mesh, w_edge, bias, *rest):
    pieces, outs, (blocks, rows) = rest[:2], rest[2 : 2 + CHUNKS], rest[-2:]

    @pl.loop(0, live[0])
    def _(group):
        for i in range(GROUP):
            block = mesh_block[group * GROUP + i]
            owner = block // 2
            flip = (owner // 2) ^ where[0]
            mine = owner % 2 == where[1]
            row = flip * HALF + (block % 2) * BLOCK

            @pl.when(mine)
            def _():
                blocks[i] = pieces[0][pl.ds(pl.multiple_of(row, BLOCK), BLOCK), :]

            @pl.when(jnp.logical_not(mine))
            def _():
                for chunk in range(CHUNKS):
                    lines = pl.ds(pl.multiple_of((3 + chunk) * GATHERED + row, BLOCK), BLOCK)
                    blocks[i, :, pl.ds(chunk * COLS, COLS)] = pieces[1][lines, :]

        first = group * GROUP * BLOCK
        for i in range(GROUP):
            at = pl.ds(pl.multiple_of(first + i * BLOCK, BLOCK), BLOCK)
            rows[pl.ds(i * BLOCK, BLOCK), :] = dot(pick[at, :], blocks[i]).astype(BF16)
        lines = pl.ds(pl.multiple_of(first, GROUP * BLOCK), GROUP * BLOCK)
        for chunk in range(CHUNKS):
            cols = pl.ds(chunk * COLS, COLS)
            outs[chunk][lines, :] = dot(rows[...], w_mesh[:, cols]) + dot(edge[lines, :], w_edge[:, cols]) + bias[:, cols]


def forward_kernel(where, live, grid_block, mesh_block, pick, recv, rest_in, *rest):
    pieces, (slope, near, far) = rest[:6], rest[6:9]
    total, blocks, sems = rest[9:]

    @pl.loop(0, live[0] * GROUP)
    def _(slot):
        mine, first, second, row = grid_place(grid_block[slot], where)
        start = first * HALF + row

        def fetch(piece, base):
            lines = pl.ds(pl.multiple_of(base + start, BLOCK), BLOCK)
            pltpu.make_async_copy(pieces[piece].at[lines, :], blocks.at[slot], sems.at[slot]).start()

        for piece in range(RING):

            @pl.when(jnp.logical_and(mine, second == piece))
            def _():
                fetch(piece, 0)

        @pl.when(jnp.logical_and(jnp.logical_not(mine), second != 2))
        def _():
            fetch(RING, jnp.minimum(second, 2) * GATHERED)

        @pl.when(jnp.logical_and(jnp.logical_not(mine), second == 2))
        def _():
            fetch(RING + 1, 0)

    total[...] = jnp.zeros_like(total)

    @pl.loop(0, live[0])
    def _(group):
        slots = [group * GROUP + i for i in range(GROUP)]
        for slot in slots:
            pltpu.make_async_copy(pieces[0].at[pl.ds(0, BLOCK), :], blocks.at[slot], sems.at[slot]).wait()
        for slot in slots:
            at = pl.ds(pl.multiple_of(slot * BLOCK, BLOCK), BLOCK)
            pre = rest_in[at, :] + dot(pick[at, :], blocks[slot])
            sig = sigmoid(pre)
            slope[at, :] = sig * (1.0 + pre * (1.0 - sig))
            value = dot(one_hot(recv, slot), (pre * sig).astype(BF16))
            mine, dz, row = mesh_place(mesh_block[slot], where)
            start = jnp.where(mine, 0, RING * HALF) + dz * HALF + row
            total[pl.ds(pl.multiple_of(start, BLOCK), BLOCK), :] += value

    near[...] = total[: RING * HALF, :]
    far[...] = total[RING * HALF :, :].astype(BF16)


def pair_sum_kernel(*refs):
    near, other, outs = refs[:CHUNKS], refs[CHUNKS : 2 * CHUNKS], refs[2 * CHUNKS :]
    for chunk in range(CHUNKS):
        for step in range(RING):
            lines = pl.ds(step * HALF, HALF)
            value = near[chunk][lines, :] + other[chunk][lines, :].astype(F32)
            outs[step][:, pl.ds(chunk * COLS, COLS)] = value.astype(outs[step].dtype)


def node_kernel(cot, w_out, own, a, b, c, aggregate, grads):
    part = own[...] + (a[...].astype(F32) + b[...].astype(F32) + c[...].astype(F32))
    total = split_dot(part, w_out[...], dot)
    aggregate[...] = total
    sig = sigmoid(total)
    grad = (cot[...] * (sig * (1.0 + total * (1.0 - sig)))).astype(BF16)
    grads[...] = dot_t(grad, w_out[...]).astype(BF16)


def zeros_kernel(*outs):
    for out in outs:
        out[...] = jnp.zeros_like(out)


def backward_kernel(where, live, grid_block, mesh_block, first_of, pick, send, *rest):
    slopes, pieces = rest[:CHUNKS], rest[CHUNKS : CHUNKS + 8]
    outs, (total, blocks) = rest[-2 - RING * CHUNKS - 2 : -2], rest[-2:]

    @pl.loop(0, live[0])
    def _(group):
        slots = [group * GROUP + i for i in range(GROUP)]
        for i, slot in enumerate(slots):
            mine, dz, row = mesh_place(mesh_block[slot], where)
            at = jnp.where(mine, dz, dz + RING)
            for piece in range(8):

                @pl.when(at == piece)
                def _():
                    blocks[i] = pieces[piece][pl.ds(pl.multiple_of(row, BLOCK), BLOCK), :]

        for i, slot in enumerate(slots):
            at = pl.ds(pl.multiple_of(slot * BLOCK, BLOCK), BLOCK)
            hot = one_hot(send, slot)
            first = first_of[slot]
            for c in range(CHUNKS):
                cols = pl.ds(c * COLS, COLS)
                grad = dot(pick[at, :], blocks[i, :, cols]) * slopes[c][at, :]
                part = dot(hot, grad.astype(BF16))
                total[first, :, cols] = jnp.where(first == slot, 0.0, total[first, :, cols]) + part

    @pl.loop(0, live[0] * GROUP)
    def _(slot):
        mine, near, far, row = grid_place(grid_block[slot], where)
        start = lax.rem(RING - near, RING) * HALF + row
        far = lax.rem(RING - far, RING)
        at = jnp.where(first_of[slot] == slot, jnp.where(mine, far, jnp.where(far == 0, RING, RING + 1)), -1)
        for step in range(RING + 2):

            @pl.when(at == step)
            def _():
                for c in range(CHUNKS):
                    if step < RING:
                        to, place = outs[RING * c + step], start
                    elif step == RING:
                        to, place = outs[-2], start + c * GATHERED
                    else:
                        to, place = outs[-1], start + (3 * c + far - 1) * GATHERED
                    to[pl.ds(pl.multiple_of(place, BLOCK), BLOCK), :] = total[slot, :, pl.ds(c * COLS, COLS)].astype(BF16)


def add(a, b):
    return (a[...].astype(F32) + b[...].astype(F32)).astype(BF16)


def merge_kernel(terms, *refs):
    into_down, into_up, out_up, out_down = refs[-4:]
    up_0, up_1, down_0, down_1 = [refs[i].at[pl.ds(base, GATHERED), :] for i, base in terms]
    out_up[:GATHERED, :] = add(up_0, into_up)
    out_up[GATHERED:, :] = up_1[...]
    out_down[:GATHERED, :] = down_0[...]
    out_down[GATHERED:, :] = add(down_1, into_down)


def column_sum_kernel(terms, *refs):
    up, down, here, *outs = refs[-6:]
    for chunk, (i, base) in enumerate(terms):
        cols = pl.ds(chunk * COLS, COLS)
        for step in range(RING):
            both = pl.ds(chunk * GATHERED + step * HALF, HALF)
            value = refs[i][pl.ds(base + step * HALF, HALF), :].astype(F32) + (up[both, :].astype(F32) + down[both, :].astype(F32))
            if step == 0:
                here[:, cols] = value
            else:
                outs[step - 1][:, cols] = value.astype(BF16)


def row_sum_kernel(w_grid, here, up, down, across, out):
    value = here[...] + (up[...].astype(F32) + down[...].astype(F32) + across[...].astype(F32))
    out[...] = split_dot(value, w_grid[...], dot_t)


def place(row, value, out, sem):
    copy = pltpu.make_async_copy(value, out.at[pl.ds(pl.multiple_of(row, HALF), HALF), :], sem)
    copy.start()
    copy.wait()


def place_other_kernel(where, value, placed, out, sem):
    place((1 - where[1]) * HALF, value, out, sem)


def place_mine_kernel(where, w_grid, here, up, down, across, out, value, sem):
    row_sum_kernel(w_grid, here, up, down, across, value)
    place(where[1] * HALF, value, out, sem)


def per_device(
    grid,
    mesh_latent,
    edge_latent,
    edge_grid_block,
    edge_mesh_block,
    sender_offset,
    receiver_offset,
    live_groups,
    w_grid,
    w_mesh,
    w_edge,
    bias,
    w_out,
    w_node,
    cotangent,
):
    def picks(offsets):
        return (offsets.reshape(-1, 1) == jnp.arange(BLOCK, dtype=jnp.int32)).astype(BF16)

    pick_send, pick_recv = picks(sender_offset), picks(receiver_offset)
    where = jnp.stack([lax.axis_index(a) for a in ("z", "core", "x", "y")]).astype(jnp.int32)
    edges = SLOTS * BLOCK
    both_chunks = range(CHUNKS)

    def call(kernel, name, outs, *args, scalars=0, scratch=(), spec=VMEM):
        whole = [SMEM] * scalars + [VMEM] * (len(args) - scalars)
        if spec is ANY:
            whole[-6:] = [ANY] * 6
        return pl.pallas_call(
            kernel,
            in_specs=whole,
            out_specs=[VMEM] * len(outs),
            out_shape=outs,
            scratch_shapes=scratch,
            compiler_params=params(),
            cost_estimate=LIGHT,
            name=name,
        )(*args)

    keep, give = call(
        first_product_kernel, "first_product", [shape(HALF, WIDTH, BF16)] * 2, where, grid, w_grid, scalars=1
    )
    got = swap(give)
    mine = jnp.concatenate([keep, got], axis=0)
    mesh_then = after(mesh_latent, mine)
    mesh_first, mesh_third = pair_z(mesh_then, 1), pair_z(mesh_then, 3)

    def far_gather(value):
        return shift(value, False, -1), shift(value, False, 1)

    def give_rows(both, up, down):
        return jnp.concatenate([both[GATHERED:], up[GATHERED:], down[GATHERED:]], axis=0)

    near = [shift(mine, True, step) for step in (-1, 2, 1)]
    ring_0, ring_1 = call(
        ring_kernel, "ring", [shape(2 * GATHERED, COLS, BF16)] * CHUNKS, keep, got, *after(near, (mesh_first, mesh_third))
    )

    mesh_far = pair_z(after(mesh_third, ring_0), 1)
    (down_0, up_0), mesh_far = lax.optimization_barrier((far_gather(ring_0), mesh_far))
    mesh_rows = jnp.concatenate([mesh_latent, mesh_first, mesh_far, mesh_third], axis=0)
    give = [give_rows(ring_0, up_0, down_0)] + [mesh_rows[:, c * COLS : (c + 1) * COLS] for c in both_chunks]
    got_0 = swap(jnp.concatenate(give, axis=0))
    across_0 = shift(up_0[:GATHERED], False, 1), shift(down_0[GATHERED:], False, -1)
    far_1 = far_gather(after(ring_1, up_0))
    edge_terms = call(
        edge_kernel,
        "edge_terms",
        [shape(edges, COLS, F32)] * CHUNKS,
        where,
        live_groups,
        edge_mesh_block,
        pick_recv,
        edge_latent,
        w_mesh,
        w_edge,
        bias.reshape(1, WIDTH),
        mesh_rows,
        got_0,
        scalars=3,
        scratch=[pltpu.VMEM((GROUP, BLOCK, WIDTH), BF16), pltpu.VMEM((GROUP * BLOCK, WIDTH), BF16)],
    )
    cot = dot_t(cotangent, w_node)

    own_across, other_across = lax.optimization_barrier(across_0)
    far_got_0 = swap(other_across)
    (down_1, up_1), edge_terms, got_0, far_got_0 = lax.optimization_barrier((far_1, edge_terms, got_0, far_got_0))
    across_1 = shift(down_1[GATHERED:], False, -1), shift(up_1[:GATHERED], False, 1)

    def forward(chunk, own, got):
        return call(
            forward_kernel,
            f"forward_{chunk}",
            [shape(edges, COLS, F32), shape(RING * HALF, COLS, F32), shape(RING * HALF, COLS, BF16)],
            where,
            live_groups,
            edge_grid_block,
            edge_mesh_block,
            pick_send,
            receiver_offset,
            edge_terms[chunk],
            *own,
            *got,
            scalars=4,
            scratch=[
                pltpu.VMEM((2 * RING * HALF, COLS), F32),
                pltpu.VMEM((SLOTS, BLOCK, COLS), BF16),
                pltpu.SemaphoreType.DMA((SLOTS,)),
            ],
            spec=ANY,
        )

    def pair_sum(*terms):
        outs = [shape(HALF, WIDTH, F32)] + [shape(HALF, WIDTH, BF16)] * 3
        return call(pair_sum_kernel, "pair_sum", outs, *terms)

    def band_sum(own, a, b, c):
        return [own, shift_z(a, 1), shift_z(c, -1), shift_z(b, 2)]

    slope_0, near_sum_0, far_sum_0 = forward(0, (ring_0, up_0, own_across, down_0), (got_0, far_got_0))
    got_1 = swap(give_rows(ring_1, up_1, down_1))
    (other_across, own_across), got_1, far_sum_0, cot = lax.optimization_barrier((across_1, got_1, far_sum_0, cot))
    far_got_1, far_sum_0 = swap(other_across), swap(far_sum_0)
    slope_1, near_sum_1, far_sum_1 = forward(
        1, (ring_1, up_1, own_across, down_1), (got_1, far_got_1)
    )
    sums = band_sum(*pair_sum(near_sum_0, near_sum_1, far_sum_0, swap(far_sum_1)))
    slopes = [slope_0, slope_1]

    aggregate, grads = call(
        node_kernel, "node", [shape(HALF, WIDTH, F32), shape(HALF, WIDTH, BF16)], cot, w_out, *sums
    )

    slots = jnp.arange(SLOTS)
    same = edge_grid_block[:, None] == edge_grid_block[None, :]
    first_of = jnp.min(jnp.where(same, slots[None, :], SLOTS), axis=1).astype(jnp.int32)

    partial_shapes = [shape(GATHERED, COLS, BF16)] * (RING * CHUNKS)
    partial_shapes += [shape(CHUNKS * GATHERED, COLS, BF16), shape(3 * CHUNKS * GATHERED, COLS, BF16)]
    zeros = call(zeros_kernel, "zeros", partial_shapes)
    up, down, across = shift_z(grads, -1), shift_z(grads, 1), shift_z(grads, 2)
    down, zeros = after((down, zeros), (up, first_of))
    band = [grads, up, across, down]
    inputs = [
        where,
        live_groups,
        edge_grid_block,
        edge_mesh_block,
        first_of,
        pick_recv,
        sender_offset,
        *slopes,
        *band,
        *[swap(p) for p in band],
    ]
    partial = pl.pallas_call(
        backward_kernel,
        in_specs=[SMEM] * 5 + [VMEM] * (len(inputs) - 5) + [VMEM] * len(zeros),
        out_specs=[VMEM] * len(zeros),
        out_shape=partial_shapes,
        input_output_aliases={len(inputs) + i: i for i in range(len(zeros))},
        scratch_shapes=[pltpu.VMEM((SLOTS, BLOCK, WIDTH), F32), pltpu.VMEM((GROUP, BLOCK, WIDTH), BF16)],
        compiler_params=params(),
        cost_estimate=LIGHT,
        name="backward",
    )(*inputs, *zeros)
    own_0, own_1, give_here, give_far = partial[:RING], partial[RING : 2 * RING], partial[-2], partial[-1]

    def far_send(into, name, terms, *refs):
        kernel = functools.partial(merge_kernel, terms)
        up, down = call(kernel, name, [shape(2 * GATHERED, COLS, BF16)] * 2, *refs, *into)
        return (shift(down, False, -1), shift(up, False, 1)), up

    def column_sum(far, name, terms, *refs):
        kernel = functools.partial(column_sum_kernel, terms)
        outs = [shape(HALF, WIDTH, F32)] + [shape(HALF, WIDTH, BF16)] * 3
        return call(kernel, name, outs, *refs, *far)

    def near_send(here, a, b, c):
        return here, shift(a, True, 1), shift(b, True, 2), shift(c, True, -1)

    def row_sum(name, terms):
        return call(row_sum_kernel, name, [shape(HALF, WIDTH, F32)], w_grid, *terms)[0]

    step = GATHERED
    into_mine = shift(own_1[2], False, -1), shift(own_0[2], False, 1)
    given = swap(give_far)
    into_other = [shift(given[step : 2 * step], False, 1), shift(given[4 * step : 5 * step], False, -1)]
    far_mine, merged = far_send(
        into_mine, "merge_mine", ((0, 0), (1, 0), (2, 0), (3, 0)), own_0[1], own_1[1], own_0[3], own_1[3]
    )
    far_other, merged = far_send(
        after(into_other, merged)[::-1], "merge_other", ((0, 0), (0, 3 * step), (0, 2 * step), (0, 5 * step)), given
    )
    given_here = swap(after(give_here, merged))
    activation = jax.nn.silu(aggregate).astype(BF16)
    mesh_out = (mesh_latent.astype(F32) + dot(activation, w_node)).astype(BF16)
    columns = column_sum(after(far_mine, (mesh_out, merged, given_here)), "column_sum_mine", ((0, 0), (1, 0)), own_0[0], own_1[0])
    near_mine = near_send(*columns)
    columns = column_sum(after(far_other, columns), "column_sum_other", ((0, 0), (0, step)), given_here)
    near_other = near_send(*columns)
    placed = pl.pallas_call(
        place_mine_kernel,
        in_specs=[SMEM] + [VMEM] * 5,
        out_specs=ANY,
        out_shape=shape(2 * HALF, WIDTH, F32),
        scratch_shapes=[pltpu.VMEM((HALF, WIDTH), F32), pltpu.SemaphoreType.DMA],
        compiler_params=params(),
        cost_estimate=LIGHT,
        name="place_mine",
    )(where, w_grid, *after(near_mine, columns))
    other = swap(row_sum("row_sum_other", after(near_other, placed)))
    grid_grad = pl.pallas_call(
        place_other_kernel,
        in_specs=[SMEM, VMEM, ANY],
        out_specs=ANY,
        out_shape=shape(2 * HALF, WIDTH, F32),
        input_output_aliases={2: 0},
        scratch_shapes=[pltpu.SemaphoreType.DMA],
        compiler_params=params(),
        cost_estimate=LIGHT,
        name="place_other",
    )(where, other, placed)
    return (mesh_out, grid_grad)


def solution(mesh):
    split = Mesh(mesh.devices.reshape(4, 2, 4, 4), ("z", "core", "x", "y"))
    rows = P(("z", "core", "x", "y"))
    placed = (rows,) * 8 + (P(),) * 6 + (rows,)
    return jax.shard_map(per_device, mesh=split, in_specs=placed, out_specs=(rows, rows), check_vma=False)
```
